32 devices in a mesh: rows: 8 (over z, y), trees: 4 (over x, core).
Axes of the slice: x: 2, y: 2, z: 4, core: 2. Of those that a mesh axis runs over, the one named last changes fastest.
Arguments:
- leaf_index: int32 [128, 65536], P(None, ('rows', 'trees')), may hold values from 0 to 31, as said below
- out_of_bag: bfloat16 [128, 65536], P(None, ('rows', 'trees')), may hold values from 0 to 4, as said below
- labels: int32 [65536], P(('rows', 'trees')), may hold values from 0 to 999
Outputs:
- tallies: float32 [128, 32, 1000], P('trees', 'rows')
- tree_error: float32 [128], P('trees')
- forest_error: float32 [], replicated
The draws below stay inside these ranges and needn't reach their ends.
Inputs may be any that keep to these rules, and one draw needn't show every extreme that they name: `out_of_bag`: 0 exactly where a row was in a tree's sample, else at least 0.25. `leaf_index`: in each tree, the 2048 rows of one device reach every leaf exactly 2048 // 32 times.
All inputs are finite; a program needn't handle non-finite values.
Results may differ from the reference program's by a relative error of at most 0.0003.
Values sent between devices are 32-bit elements; how exact they have to be, the bound alone decides.
A program may use at most 128 MiB of HBM per device.

```python
import math
import jax
import jax.numpy as jnp
from jax import lax

TREES = 128
CLASSES = 1000
LEAVES = 32
ROW_DEV = 2048
ROWS = 65536


def label_leaf_pair(key):
    device_total = ROWS // ROW_DEV
    per_leaf = ROW_DEV // LEAVES
    class_weight = (1 << 20) // (jnp.arange(CLASSES, dtype=jnp.int32) + 1)
    bounds = jnp.cumsum(class_weight).astype(jnp.int32)
    drawn_value = jax.random.randint(jax.random.fold_in(key, 3), (ROWS,), 0, bounds[-1], dtype=jnp.int32)
    rank_class = jnp.searchsorted(bounds, drawn_value, side='right').astype(jnp.int32)
    class_order = jax.random.permutation(jax.random.fold_in(key, 5), CLASSES).astype(jnp.int32)
    labels = jnp.take(class_order, rank_class).astype(jnp.int32)
    tie_keys = jax.random.split(jax.random.fold_in(key, 7), TREES * device_total)
    positions = jnp.arange(ROW_DEV, dtype=jnp.int32)
    shuffled = jax.vmap(lambda single: jax.random.permutation(single, positions))(tie_keys)
    shuffled = shuffled.reshape(TREES, device_total, ROW_DEV).astype(jnp.int32)
    random_leaf = shuffled % LEAVES
    sort_score = labels.reshape(1, device_total, ROW_DEV) * ROW_DEV + shuffled
    sort_order = jnp.argsort(sort_score, axis=2, stable=True).astype(jnp.int32)
    row_rank = jnp.argsort(sort_order, axis=2, stable=True).astype(jnp.int32)
    leaf_keys = jax.random.split(jax.random.fold_in(key, 9), TREES)
    leaf_maps = jax.vmap(lambda single: jax.random.permutation(single, LEAVES))(leaf_keys).astype(jnp.int32)
    sorted_leaf = jax.vmap(lambda mapping, ranks: jnp.take(mapping, ranks // per_leaf))(leaf_maps, row_rank)
    picked = jax.random.permutation(jax.random.fold_in(key, 13), TREES) < TREES // 2
    leaf_final = jnp.where(picked[:, None, None], sorted_leaf, random_leaf)
    return (labels, leaf_final.reshape(TREES, ROWS).astype(jnp.int32))


def draw_labels(key, part):
    return label_leaf_pair(key)[0]


def draw_leaf_index(key, part):
    return label_leaf_pair(key)[1]


def draw_out_of_bag(key, part):
    marks_drawn = jax.random.randint(jax.random.fold_in(key, 11), (TREES, ROWS), 0, 1000, dtype=jnp.int32)
    position = jnp.arange(ROWS, dtype=jnp.int32)
    level = 200 + 400 * position // ROWS
    sizes = jnp.exp(jax.random.uniform(jax.random.fold_in(key, 17), (TREES, ROWS), jnp.float32, math.log(0.25), math.log(4.0)))
    return jnp.where(marks_drawn < level[None, :], sizes, 0.0).astype(jnp.bfloat16)


def setup_inputs(seed: int = 0) -> dict:
    arg_keys = jax.random.split(jax.random.key(seed), 4)
    leaf_index = draw_leaf_index(jax.random.fold_in(arg_keys[3], 71), 0)
    out_of_bag = draw_out_of_bag(jax.random.fold_in(arg_keys[3], 71), 0)
    labels = draw_labels(jax.random.fold_in(arg_keys[3], 71), 0)
    return {"leaf_index": leaf_index, "out_of_bag": out_of_bag, "labels": labels}


def reference(leaf_index, out_of_bag, labels):
    def one_tree(tree_pair):
        leaves_row, weight_row = tree_pair
        slot_index = leaves_row * CLASSES + labels
        counts = jax.ops.segment_sum(weight_row.astype(jnp.float32), slot_index, num_segments=LEAVES * CLASSES)
        return counts.reshape(LEAVES, CLASSES)

    tallies = lax.map(one_tree, (leaf_index, out_of_bag))
    leaf_total = jnp.sum(tallies, axis=2)
    leaf_top = jnp.max(tallies, axis=2)
    wrong_sum = jnp.sum(leaf_total - leaf_top, axis=1)
    seen_sum = jnp.sum(leaf_total, axis=1)
    tree_error = wrong_sum / seen_sum
    forest_error = jnp.sum(wrong_sum) / jnp.sum(seen_sum)
    return tallies, tree_error, forest_error
```

```python
import functools

import jax
import jax.numpy as jnp
from jax import lax
from jax.experimental import pallas as pl
from jax.experimental.pallas import tpu as pltpu
from jax.sharding import PartitionSpec as P

CLASSES = 1000
LEAVES = 32
LANES = 128
CHUNK = 256


def nt_dot(a, b):
    return lax.dot_general(a, b, (((1,), (1,)), ((), ())), preferred_element_type=jnp.float32)


def compact_tree(leaf_ref, weight_ref, hi_ref, lo_ref, tri_ref, t, rows, slots):
    leaf = leaf_ref[pl.ds(t, 1), :]
    weight = weight_ref[pl.ds(t, 1), :]
    chunks = rows // CHUNK
    leaf_ids = lax.broadcasted_iota(jnp.int32, (LEAVES, CHUNK), 0)
    masks = [leaf[:, c * CHUNK:(c + 1) * CHUNK] == leaf_ids for c in range(chunks)]
    ones = [jnp.where(m, 1.0, 0.0) for m in masks]
    stacked = jnp.concatenate(ones, axis=0).astype(jnp.bfloat16)
    counts = jnp.dot(stacked, tri_ref[...], preferred_element_type=jnp.float32)
    carry = jnp.zeros((LEAVES, 1), jnp.float32)
    slot_ids = lax.broadcasted_iota(jnp.int32, (slots, CHUNK), 0).astype(jnp.float32)
    placed, slot_hot = [], []
    for c in range(chunks):
        running = counts[c * LEAVES:(c + 1) * LEAVES] + carry
        carry = running[:, CHUNK - 1:]
        rank = jnp.sum(jnp.where(masks[c], running, 0.0), axis=0, keepdims=True) - 1.0
        slot_hot.append(jnp.where(rank == slot_ids, 1.0, 0.0).astype(jnp.bfloat16))
        cols = slice(c * CHUNK, (c + 1) * CHUNK)
        w = jnp.where(masks[c], weight[:, cols], 0.0).astype(jnp.bfloat16)
        one = stacked[c * LEAVES:(c + 1) * LEAVES]
        placed.append(jnp.concatenate([w, one * hi_ref[:, cols], one * lo_ref[:, cols]], axis=0))
    out = nt_dot(jnp.concatenate(placed, axis=1), jnp.concatenate(slot_hot, axis=1))
    classes = out[LEAVES:2 * LEAVES] + out[2 * LEAVES:]
    return jnp.concatenate([out[:LEAVES], classes], axis=1)


def compact_kernel(n_rows, leaf_ref, bag_ref, label_ref, send_ref, weight_ref, hi_ref, lo_ref, tri_ref):
    trees, rows = leaf_ref.shape
    slots = rows // LEAVES
    leaf_block = LEAVES // n_rows
    group = max(8 // leaf_block, 2)
    labels = label_ref[...]
    hi = (labels >> 5) << 5
    hi_ref[...] = jnp.broadcast_to(hi.astype(jnp.float32), (LEAVES, rows)).astype(jnp.bfloat16)
    lo_ref[...] = jnp.broadcast_to((labels - hi).astype(jnp.float32), (LEAVES, rows)).astype(jnp.bfloat16)
    r = lax.broadcasted_iota(jnp.int32, (CHUNK, CHUNK), 0)
    c = lax.broadcasted_iota(jnp.int32, (CHUNK, CHUNK), 1)
    tri_ref[...] = jnp.where(r <= c, 1.0, 0.0).astype(jnp.bfloat16)
    weight_ref[...] = bag_ref[...].astype(jnp.float32)

    def step(i, _):
        parts = [
            compact_tree(leaf_ref, weight_ref, hi_ref, lo_ref, tri_ref, i * group + j, rows, slots)
            for j in range(group)
        ]
        size = group * leaf_block
        for b in range(n_rows):
            tile = jnp.concatenate([p[b * leaf_block:(b + 1) * leaf_block] for p in parts], axis=0)
            send_ref[b, pl.ds(pl.multiple_of(i * size, size), size), :] = tile
        return 0

    lax.fori_loop(0, trees // group, step, 0)


def compact(leaf_index, out_of_bag, labels, n_rows):
    trees, rows = leaf_index.shape
    vmem = pl.BlockSpec(memory_space=pltpu.VMEM)
    return pl.pallas_call(
        functools.partial(compact_kernel, n_rows),
        out_shape=jax.ShapeDtypeStruct((n_rows, trees * (LEAVES // n_rows), LANES), jnp.float32),
        in_specs=[vmem] * 3,
        out_specs=vmem,
        scratch_shapes=[
            pltpu.VMEM((trees, rows), jnp.float32),
            pltpu.VMEM((LEAVES, rows), jnp.bfloat16),
            pltpu.VMEM((LEAVES, rows), jnp.bfloat16),
            pltpu.VMEM((CHUNK, CHUNK), jnp.bfloat16),
        ],
        compiler_params=pltpu.CompilerParams(vmem_limit_bytes=48 << 20),
        name="compact",
    )(leaf_index, out_of_bag, labels.reshape(1, rows))


def tally_kernel(recv_ref, tally_ref):
    sources, cells, _ = recv_ref.shape
    pairs = sources // 2
    high = tally_ref.shape[1]
    low_half = lax.broadcasted_iota(jnp.int32, (pairs, 8, LANES), 2) < LANES // 2
    lo_ids = lax.broadcasted_iota(jnp.int32, (LANES, LANES), 0)
    hi_ids = lax.broadcasted_iota(jnp.int32, (high, LANES), 0)

    def step(i, _):
        block = recv_ref[:, pl.ds(pl.multiple_of(i * 8, 8), 8), :]
        block = block.reshape(pairs, 2, 8, LANES)
        first, second = block[:, 0], block[:, 1]
        turned_first = pltpu.roll(first, LANES // 2, 2)
        turned_second = pltpu.roll(second, LANES // 2, 2)
        weight = jnp.where(low_half, first, turned_second)
        label = jnp.where(low_half, turned_first, second).astype(jnp.int32)
        hi, lo = label >> 7, label & (LANES - 1)
        for j in range(8):
            a, b = [], []
            for p in range(pairs):
                a.append(jnp.where(hi[p, j:j + 1] == hi_ids, weight[p, j:j + 1], 0.0))
                b.append(jnp.where(lo[p, j:j + 1] == lo_ids, 1.0, 0.0).astype(jnp.bfloat16))
            a = jnp.concatenate(a, axis=1).astype(jnp.bfloat16)
            tally_ref[i * 8 + j] = nt_dot(a, jnp.concatenate(b, axis=1))
        return 0

    lax.fori_loop(0, cells // 8, step, 0)


def tally(recv):
    sources, cells, _ = recv.shape
    high = pl.cdiv(CLASSES, LANES)
    vmem = pl.BlockSpec(memory_space=pltpu.VMEM)
    return pl.pallas_call(
        tally_kernel,
        out_shape=jax.ShapeDtypeStruct((cells, high, LANES), jnp.float32),
        in_specs=[vmem],
        out_specs=vmem,
        compiler_params=pltpu.CompilerParams(vmem_limit_bytes=48 << 20),
        name="tally",
    )(recv)


def per_device(leaf_index, out_of_bag, labels):
    n_rows = lax.axis_size("rows")
    tree_count = lax.axis_size("trees")
    trees = leaf_index.shape[0]
    tree_block = trees // tree_count
    leaf_block = LEAVES // n_rows
    cells = tree_block * leaf_block
    send = compact(leaf_index, out_of_bag, labels, n_rows)
    send = send.reshape(n_rows * tree_count, cells, LANES)
    recv = lax.all_to_all(send, ("rows", "trees"), split_axis=0, concat_axis=0, tiled=True)
    table = tally(recv).reshape(cells, -1)
    tallies = table[:, :CLASSES].reshape(tree_block, leaf_block, CLASSES)
    leaf_total = jnp.sum(tallies, axis=2)
    leaf_top = jnp.max(tallies, axis=2)
    local = jnp.stack([jnp.sum(leaf_total - leaf_top, axis=1), jnp.sum(leaf_total, axis=1)])
    mine = lax.axis_index("trees") * tree_block
    spread = lax.dynamic_update_slice(jnp.zeros((2, trees), jnp.float32), local, (0, mine))
    sums = lax.psum(spread, ("rows", "trees"))
    own = lax.dynamic_slice(sums, (0, mine), (2, tree_block))
    tree_error = own[0] / own[1]
    pooled = jnp.sum(sums, axis=1)
    return tallies, tree_error, pooled[0] / pooled[1]


def solution(mesh):
    in_specs = (P(None, ("rows", "trees")), P(None, ("rows", "trees")), P(("rows", "trees")))
    out_specs = (P("trees", "rows", None), P("trees"), P())
    return jax.shard_map(
        per_device, mesh=mesh, in_specs=in_specs, out_specs=out_specs, check_vma=False
    )
```

```python
import functools

import jax
import jax.numpy as jnp
from jax import lax
from jax.experimental import pallas as pl
from jax.experimental.pallas import tpu as pltpu
from jax.sharding import PartitionSpec as P

CLASSES = 1000
LEAVES = 32
LANES = 128
CHUNK = 256


def nt_dot(a, b):
    return lax.dot_general(a, b, (((1,), (1,)), ((), ())), preferred_element_type=jnp.float32)


def compact_tree(leaf_ref, weight_ref, hi_ref, lo_ref, tri_ref, t, rows, slots):
    leaf = leaf_ref[pl.ds(t, 1), :]
    weight = weight_ref[pl.ds(t, 1), :]
    chunks = rows // CHUNK
    leaf_ids = lax.broadcasted_iota(jnp.int32, (LEAVES, CHUNK), 0)
    masks = [leaf[:, c * CHUNK:(c + 1) * CHUNK] == leaf_ids for c in range(chunks)]
    ones = [jnp.where(m, 1.0, 0.0) for m in masks]
    stacked = jnp.concatenate(ones, axis=0).astype(jnp.bfloat16)
    counts = jnp.dot(stacked, tri_ref[...], preferred_element_type=jnp.float32)
    carry = jnp.zeros((LEAVES, 1), jnp.float32)
    slot_ids = lax.broadcasted_iota(jnp.int32, (slots, CHUNK), 0).astype(jnp.float32)
    placed, slot_hot = [], []
    for c in range(chunks):
        running = counts[c * LEAVES:(c + 1) * LEAVES] + carry
        carry = running[:, CHUNK - 1:]
        rank = jnp.sum(jnp.where(masks[c], running, 0.0), axis=0, keepdims=True) - 1.0
        slot_hot.append(jnp.where(rank == slot_ids, 1.0, 0.0).astype(jnp.bfloat16))
        cols = slice(c * CHUNK, (c + 1) * CHUNK)
        w = jnp.where(masks[c], weight[:, cols], 0.0).astype(jnp.bfloat16)
        one = stacked[c * LEAVES:(c + 1) * LEAVES]
        placed.append(jnp.concatenate([w, one * hi_ref[:, cols], one * lo_ref[:, cols]], axis=0))
    out = nt_dot(jnp.concatenate(placed, axis=1), jnp.concatenate(slot_hot, axis=1))
    classes = out[LEAVES:2 * LEAVES] + out[2 * LEAVES:]
    return jnp.concatenate([out[:LEAVES], classes], axis=1)


def others(n, me, body):
    lax.fori_loop(1, n, lambda k, _: body(lax.rem(me + k, n)) or 0, 0)


def greet_all(n, tree_count, me):
    barrier = pltpu.get_barrier_semaphore()

    def greet(other):
        pl.semaphore_signal(
            barrier, inc=1, device_id=(other // tree_count, lax.rem(other, tree_count)),
            device_id_type=pl.DeviceIdType.MESH,
        )

    others(n, me, greet)
    return lambda: pl.semaphore_wait(barrier, n - 1)


def compact_kernel(n_rows, tree_count, leaf_ref, bag_ref, label_ref, recv_ref, send_ref, weight_ref,
                   hi_ref, lo_ref, tri_ref, send_sem, recv_sem, own_sem):
    trees, rows = leaf_ref.shape
    slots = rows // LEAVES
    leaf_block = LEAVES // n_rows
    group = max(8 // leaf_block, 2)
    size = group * leaf_block
    tree_block = trees // tree_count
    n = n_rows * tree_count
    my_row, my_tree = lax.axis_index("rows"), lax.axis_index("trees")
    me = my_row * tree_count + my_tree
    wait_all = greet_all(n, tree_count, me)

    labels = label_ref[...]
    hi = (labels >> 5) << 5
    hi_ref[...] = jnp.broadcast_to(hi.astype(jnp.float32), (LEAVES, rows)).astype(jnp.bfloat16)
    lo_ref[...] = jnp.broadcast_to((labels - hi).astype(jnp.float32), (LEAVES, rows)).astype(jnp.bfloat16)
    r = lax.broadcasted_iota(jnp.int32, (CHUNK, CHUNK), 0)
    c = lax.broadcasted_iota(jnp.int32, (CHUNK, CHUNK), 1)
    tri_ref[...] = jnp.where(r <= c, 1.0, 0.0).astype(jnp.bfloat16)
    weight_ref[...] = bag_ref[...].astype(jnp.float32)

    def transfer(block, slot, other):
        return pltpu.make_async_remote_copy(
            src_ref=send_ref.at[block],
            dst_ref=recv_ref.at[slot],
            send_sem=send_sem.at[block],
            recv_sem=recv_sem.at[slot],
            device_id=(other // tree_count, lax.rem(other, tree_count)),
            device_id_type=pl.DeviceIdType.MESH,
        )

    def phase(tt):
        def step(i, _):
            parts = [
                compact_tree(leaf_ref, weight_ref, hi_ref, lo_ref, tri_ref,
                             tt * tree_block + i * group + j, rows, slots)
                for j in range(group)
            ]
            for b in range(n_rows):
                tile = jnp.concatenate([p[b * leaf_block:(b + 1) * leaf_block] for p in parts], axis=0)
                send_ref[b * tree_count + tt, pl.ds(pl.multiple_of(i * size, size), size), :] = tile
            return 0

        lax.fori_loop(0, tree_block // group, step, 0)

    def send(k, tt):
        other = lax.rem(my_row + k, n_rows) * tree_count + tt
        transfer(other, me, other).start()

    def away(i, _):
        tt = lax.rem(my_tree + i, tree_count)
        phase(tt)
        lax.fori_loop(0, n_rows, lambda k, _: send(k, tt) or 0, 0)
        return 0

    wait_all()
    lax.fori_loop(1, tree_count, away, 0)
    phase(my_tree)
    lax.fori_loop(1, n_rows, lambda k, _: send(k, my_tree) or 0, 0)
    own = pltpu.make_async_copy(send_ref.at[me], recv_ref.at[me], own_sem)
    own.start()
    others(n, me, lambda other: transfer(other, other, other).wait())
    own.wait()


def compact(leaf_index, out_of_bag, labels, n_rows, tree_count):
    trees, rows = leaf_index.shape
    n = n_rows * tree_count
    cells = (trees // tree_count) * (LEAVES // n_rows)
    vmem = pl.BlockSpec(memory_space=pltpu.VMEM)
    return pl.pallas_call(
        functools.partial(compact_kernel, n_rows, tree_count),
        out_shape=jax.ShapeDtypeStruct((n, cells, LANES), jnp.float32),
        in_specs=[vmem] * 3,
        out_specs=pl.BlockSpec(memory_space=pl.ANY),
        scratch_shapes=[
            pltpu.VMEM((n, cells, LANES), jnp.float32),
            pltpu.VMEM((trees, rows), jnp.float32),
            pltpu.VMEM((LEAVES, rows), jnp.bfloat16),
            pltpu.VMEM((LEAVES, rows), jnp.bfloat16),
            pltpu.VMEM((CHUNK, CHUNK), jnp.bfloat16),
            pltpu.SemaphoreType.DMA((n,)),
            pltpu.SemaphoreType.DMA((n,)),
            pltpu.SemaphoreType.DMA,
        ],
        compiler_params=pltpu.CompilerParams(
            vmem_limit_bytes=48 << 20, collective_id=0, has_side_effects=True
        ),
        name="compact",
    )(leaf_index, out_of_bag, labels.reshape(1, rows))


def rates_kernel(n_rows, tree_count, local_ref, out_ref, recv_ref, send_sem, recv_sem):
    n = n_rows * tree_count
    my_row, my_tree = lax.axis_index("rows"), lax.axis_index("trees")
    me = my_row * tree_count + my_tree
    wait_all = greet_all(n, tree_count, me)
    wait_all()

    def transfer(slot, other):
        return pltpu.make_async_remote_copy(
            src_ref=local_ref,
            dst_ref=recv_ref.at[slot],
            send_sem=send_sem.at[other],
            recv_sem=recv_sem.at[slot],
            device_id=(other // tree_count, lax.rem(other, tree_count)),
            device_id_type=pl.DeviceIdType.MESH,
        )

    others(n, me, lambda other: transfer(me, other).start())
    recv_ref[me] = local_ref[...]
    others(n, me, lambda other: transfer(other, other).wait())
    mine = jnp.zeros((8, LANES), jnp.float32)
    total = jnp.zeros((8, LANES), jnp.float32)
    for row in range(n_rows):
        mine += recv_ref[row * tree_count + my_tree]
    for device in range(n):
        total += recv_ref[device]
    pooled = jnp.sum(total, axis=1, keepdims=True)
    out_ref[0:1] = mine[0:1] / jnp.where(mine[2:3] > 0, mine[1:2], 1.0)
    out_ref[1:2] = jnp.broadcast_to(pooled[0:1] / pooled[1:2], (1, LANES))
    out_ref[2:] = jnp.zeros((6, LANES), jnp.float32)


def rates(local, n_rows, tree_count):
    n = n_rows * tree_count
    vmem = pl.BlockSpec(memory_space=pltpu.VMEM)
    return pl.pallas_call(
        functools.partial(rates_kernel, n_rows, tree_count),
        out_shape=jax.ShapeDtypeStruct((8, LANES), jnp.float32),
        in_specs=[vmem],
        out_specs=vmem,
        scratch_shapes=[
            pltpu.VMEM((n, 8, LANES), jnp.float32),
            pltpu.SemaphoreType.DMA((n,)),
            pltpu.SemaphoreType.DMA((n,)),
        ],
        compiler_params=pltpu.CompilerParams(collective_id=1, has_side_effects=True),
        name="rates",
    )(local)


def tally_kernel(leaf_block, recv_ref, tally_ref, sums_ref):
    sources, cells, _ = recv_ref.shape
    pairs = sources // 2
    high = tally_ref.shape[1]
    low_half = lax.broadcasted_iota(jnp.int32, (pairs, 8, LANES), 2) < LANES // 2
    lo_ids = lax.broadcasted_iota(jnp.int32, (LANES, LANES), 0)
    hi_ids = lax.broadcasted_iota(jnp.int32, (high, LANES), 0)

    def step(i, _):
        block = recv_ref[:, pl.ds(pl.multiple_of(i * 8, 8), 8), :]
        block = block.reshape(pairs, 2, 8, LANES)
        first, second = block[:, 0], block[:, 1]
        turned_first = pltpu.roll(first, LANES // 2, 2)
        turned_second = pltpu.roll(second, LANES // 2, 2)
        weight = jnp.where(low_half, first, turned_second)
        label = jnp.where(low_half, turned_first, second).astype(jnp.int32)
        hi, lo = label >> 7, label & (LANES - 1)
        for j in range(8):
            a, b = [], []
            for p in range(pairs):
                a.append(jnp.where(hi[p, j:j + 1] == hi_ids, weight[p, j:j + 1], 0.0))
                b.append(jnp.where(lo[p, j:j + 1] == lo_ids, 1.0, 0.0).astype(jnp.bfloat16))
            a = jnp.concatenate(a, axis=1).astype(jnp.bfloat16)
            tally_ref[i * 8 + j] = nt_dot(a, jnp.concatenate(b, axis=1))
        return 0

    lax.fori_loop(0, cells // 8, step, 0)
    table = tally_ref[...]
    seen = jnp.sum(jnp.sum(table, axis=1), axis=1, keepdims=True)
    top = jnp.max(jnp.max(table, axis=1), axis=1, keepdims=True)
    tree = lax.broadcasted_iota(jnp.int32, (cells, LANES), 0) // leaf_block
    held = tree == lax.broadcasted_iota(jnp.int32, (cells, LANES), 1)
    sums_ref[...] = jnp.zeros((8, LANES), jnp.float32)
    sums_ref[0:1] = jnp.sum(jnp.where(held, seen - top, 0.0), axis=0, keepdims=True)
    sums_ref[1:2] = jnp.sum(jnp.where(held, seen, 0.0), axis=0, keepdims=True)
    sums_ref[2:3] = jnp.sum(jnp.where(held, 1.0, 0.0), axis=0, keepdims=True)


def tally(recv, leaf_block):
    sources, cells, _ = recv.shape
    high = pl.cdiv(CLASSES, LANES)
    vmem = pl.BlockSpec(memory_space=pltpu.VMEM)
    return pl.pallas_call(
        functools.partial(tally_kernel, leaf_block),
        out_shape=[
            jax.ShapeDtypeStruct((cells, high, LANES), jnp.float32),
            jax.ShapeDtypeStruct((8, LANES), jnp.float32),
        ],
        in_specs=[vmem],
        out_specs=[vmem, vmem],
        compiler_params=pltpu.CompilerParams(vmem_limit_bytes=48 << 20),
        name="tally",
    )(recv)


def per_device(leaf_index, out_of_bag, labels):
    n_rows = lax.axis_size("rows")
    tree_count = lax.axis_size("trees")
    trees = leaf_index.shape[0]
    tree_block = trees // tree_count
    leaf_block = LEAVES // n_rows
    cells = tree_block * leaf_block
    recv = compact(leaf_index, out_of_bag, labels, n_rows, tree_count)
    table, sums = tally(recv, leaf_block)
    tallies = table.reshape(cells, -1)[:, :CLASSES].reshape(tree_block, leaf_block, CLASSES)
    result = rates(sums, n_rows, tree_count)
    return tallies, result[0, :tree_block], result[1, 0]


def solution(mesh):
    in_specs = (P(None, ("rows", "trees")), P(None, ("rows", "trees")), P(("rows", "trees")))
    out_specs = (P("trees", "rows", None), P("trees"), P())
    return jax.shard_map(
        per_device, mesh=mesh, in_specs=in_specs, out_specs=out_specs, check_vma=False
    )
```

```python
import functools

import jax
import jax.numpy as jnp
from jax import lax
from jax.experimental import pallas as pl
from jax.experimental.pallas import tpu as pltpu
from jax.sharding import PartitionSpec as P

CLASSES = 1000
LEAVES = 32
LANES = 128
CHUNK = 256
GROUP = 4


def nt_dot(a, b):
    return lax.dot_general(a, b, (((1,), (1,)), ((), ())), preferred_element_type=jnp.float32)


def rows16(row):
    return jnp.broadcast_to(row, (16, row.shape[1])).astype(jnp.bfloat16)


def ids16(first, width):
    return (lax.broadcasted_iota(jnp.int32, (16, width), 0) + first).astype(jnp.float32).astype(jnp.bfloat16)


def compact_group(group, leaf_ref, weight_ref, hi_ref, lo_ref, tri_ref, mask_ref, hot_ref, placed_ref, first, slots):
    rows = leaf_ref.shape[1]
    chunks = rows // CHUNK
    one, zero = jnp.ones((), jnp.bfloat16), jnp.zeros((), jnp.bfloat16)
    leaf_ids = [ids16(q * 16, CHUNK) for q in range(LEAVES // 16)]
    slot_ids = [ids16(q * 16, CHUNK) for q in range(slots // 16)]
    leaf_ids32 = lax.broadcasted_iota(jnp.int32, (LEAVES, CHUNK), 0)
    for j in range(group):
        for c in range(chunks):
            cols = slice(c * CHUNK, (c + 1) * CHUNK)
            leaf = rows16(leaf_ref[pl.ds(first + j, 1), cols].astype(jnp.float32))
            weight = rows16(weight_ref[pl.ds(first + j, 1), cols])
            for q in range(LEAVES // 16):
                mask = leaf == leaf_ids[q]
                at = (j * chunks + c) * LEAVES + q * 16
                mask_ref[at:at + 16, :] = jnp.where(mask, one, zero)
                at = j * 3 * LEAVES + q * 16
                placed_ref[at:at + 16, cols] = jnp.where(mask, weight, zero)
                placed_ref[at + LEAVES:at + LEAVES + 16, cols] = jnp.where(mask, hi_ref[:, cols], zero)
                placed_ref[at + 2 * LEAVES:at + 2 * LEAVES + 16, cols] = jnp.where(mask, lo_ref[:, cols], zero)
    counts = jnp.dot(mask_ref[...], tri_ref[...], preferred_element_type=jnp.float32)
    for j in range(group):
        carry = jnp.zeros((LEAVES, 1), jnp.float32)
        for c in range(chunks):
            cols = slice(c * CHUNK, (c + 1) * CHUNK)
            at = (j * chunks + c) * LEAVES
            running = counts[at:at + LEAVES] + carry
            carry = running[:, CHUNK - 1:]
            mask = leaf_ref[pl.ds(first + j, 1), cols] == leaf_ids32
            rank = rows16(jnp.sum(jnp.where(mask, running, 0.0), axis=0, keepdims=True) - 1.0)
            for q in range(slots // 16):
                at = j * slots + q * 16
                hot_ref[at:at + 16, cols] = jnp.where(rank == slot_ids[q], one, zero)
    out = nt_dot(placed_ref[...], hot_ref[...])
    parts = []
    for j in range(group):
        mine = out[j * 3 * LEAVES:(j + 1) * 3 * LEAVES, j * slots:(j + 1) * slots]
        classes = mine[LEAVES:2 * LEAVES] + mine[2 * LEAVES:]
        parts.append(jnp.concatenate([mine[:LEAVES], classes], axis=1))
    return parts


def others(n, me, body):
    lax.fori_loop(1, n, lambda k, _: body(lax.rem(me + k, n)) or 0, 0)


def greet_all(n, tree_count, me):
    barrier = pltpu.get_barrier_semaphore()

    def greet(other):
        pl.semaphore_signal(
            barrier, inc=1, device_id=(other // tree_count, lax.rem(other, tree_count)),
            device_id_type=pl.DeviceIdType.MESH,
        )

    others(n, me, greet)
    return lambda: pl.semaphore_wait(barrier, n - 1)


def compact_kernel(n_rows, tree_count, leaf_ref, bag_ref, label_ref, recv_ref, send_ref, weight_ref,
                   hi_ref, lo_ref, tri_ref, mask_ref, hot_ref, placed_ref, send_sem, recv_sem, own_sem):
    trees, rows = leaf_ref.shape
    slots = rows // LEAVES
    leaf_block = LEAVES // n_rows
    group = GROUP
    size = group * leaf_block
    tree_block = trees // tree_count
    n = n_rows * tree_count
    my_row, my_tree = lax.axis_index("rows"), lax.axis_index("trees")
    me = my_row * tree_count + my_tree
    wait_all = greet_all(n, tree_count, me)

    labels = label_ref[...]
    hi = (labels >> 5) << 5
    hi_ref[...] = rows16(hi.astype(jnp.float32))
    lo_ref[...] = rows16((labels - hi).astype(jnp.float32))
    r = lax.broadcasted_iota(jnp.int32, (CHUNK, CHUNK), 0)
    c = lax.broadcasted_iota(jnp.int32, (CHUNK, CHUNK), 1)
    tri_ref[...] = jnp.where(r <= c, 1.0, 0.0).astype(jnp.bfloat16)
    weight_ref[...] = bag_ref[...].astype(jnp.float32)

    def transfer(block, slot, other):
        return pltpu.make_async_remote_copy(
            src_ref=send_ref.at[block],
            dst_ref=recv_ref.at[slot],
            send_sem=send_sem.at[block],
            recv_sem=recv_sem.at[slot],
            device_id=(other // tree_count, lax.rem(other, tree_count)),
            device_id_type=pl.DeviceIdType.MESH,
        )

    def phase(tt):
        def step(i, _):
            parts = compact_group(group, leaf_ref, weight_ref, hi_ref, lo_ref, tri_ref, mask_ref, hot_ref,
                                  placed_ref, tt * tree_block + i * group, slots)
            for b in range(n_rows):
                tile = jnp.concatenate([p[b * leaf_block:(b + 1) * leaf_block] for p in parts], axis=0)
                send_ref[b * tree_count + tt, pl.ds(pl.multiple_of(i * size, size), size), :] = tile
            return 0

        lax.fori_loop(0, tree_block // group, step, 0)

    def send(k, tt):
        other = lax.rem(my_row + k, n_rows) * tree_count + tt
        transfer(other, me, other).start()

    def away(i, _):
        tt = lax.rem(my_tree + i, tree_count)
        phase(tt)
        lax.fori_loop(0, n_rows, lambda k, _: send(k, tt) or 0, 0)
        return 0

    wait_all()
    lax.fori_loop(1, tree_count, away, 0)
    phase(my_tree)
    lax.fori_loop(1, n_rows, lambda k, _: send(k, my_tree) or 0, 0)
    own = pltpu.make_async_copy(send_ref.at[me], recv_ref.at[me], own_sem)
    own.start()
    others(n, me, lambda other: transfer(other, other, other).wait())
    own.wait()


def compact(leaf_index, out_of_bag, labels, n_rows, tree_count):
    trees, rows = leaf_index.shape
    n = n_rows * tree_count
    cells = (trees // tree_count) * (LEAVES // n_rows)
    vmem = pl.BlockSpec(memory_space=pltpu.VMEM)
    return pl.pallas_call(
        functools.partial(compact_kernel, n_rows, tree_count),
        out_shape=jax.ShapeDtypeStruct((n, cells, LANES), jnp.float32),
        in_specs=[vmem] * 3,
        out_specs=pl.BlockSpec(memory_space=pl.ANY),
        scratch_shapes=[
            pltpu.VMEM((n, cells, LANES), jnp.float32),
            pltpu.VMEM((trees, rows), jnp.float32),
            pltpu.VMEM((16, rows), jnp.bfloat16),
            pltpu.VMEM((16, rows), jnp.bfloat16),
            pltpu.VMEM((CHUNK, CHUNK), jnp.bfloat16),
            pltpu.VMEM((GROUP * LEAVES * (rows // CHUNK), CHUNK), jnp.bfloat16),
            pltpu.VMEM((GROUP * (rows // LEAVES), rows), jnp.bfloat16),
            pltpu.VMEM((GROUP * 3 * LEAVES, rows), jnp.bfloat16),
            pltpu.SemaphoreType.DMA((n,)),
            pltpu.SemaphoreType.DMA((n,)),
            pltpu.SemaphoreType.DMA,
        ],
        compiler_params=pltpu.CompilerParams(
            vmem_limit_bytes=48 << 20, collective_id=0, has_side_effects=True
        ),
        name="compact",
    )(leaf_index, out_of_bag, labels.reshape(1, rows))


def rates_kernel(n_rows, tree_count, local_ref, out_ref, recv_ref, send_sem, recv_sem):
    n = n_rows * tree_count
    my_row, my_tree = lax.axis_index("rows"), lax.axis_index("trees")
    me = my_row * tree_count + my_tree
    wait_all = greet_all(n, tree_count, me)
    wait_all()

    def transfer(slot, other):
        return pltpu.make_async_remote_copy(
            src_ref=local_ref,
            dst_ref=recv_ref.at[slot],
            send_sem=send_sem.at[other],
            recv_sem=recv_sem.at[slot],
            device_id=(other // tree_count, lax.rem(other, tree_count)),
            device_id_type=pl.DeviceIdType.MESH,
        )

    others(n, me, lambda other: transfer(me, other).start())
    recv_ref[me] = local_ref[...]
    others(n, me, lambda other: transfer(other, other).wait())
    mine = jnp.zeros((8, LANES), jnp.float32)
    total = jnp.zeros((8, LANES), jnp.float32)
    for row in range(n_rows):
        mine += recv_ref[row * tree_count + my_tree]
    for device in range(n):
        total += recv_ref[device]
    pooled = jnp.sum(total, axis=1, keepdims=True)
    out_ref[0:1] = mine[0:1] / jnp.where(mine[2:3] > 0, mine[1:2], 1.0)
    out_ref[1:2] = jnp.broadcast_to(pooled[0:1] / pooled[1:2], (1, LANES))
    out_ref[2:] = jnp.zeros((6, LANES), jnp.float32)


def rates(local, n_rows, tree_count):
    n = n_rows * tree_count
    vmem = pl.BlockSpec(memory_space=pltpu.VMEM)
    return pl.pallas_call(
        functools.partial(rates_kernel, n_rows, tree_count),
        out_shape=jax.ShapeDtypeStruct((8, LANES), jnp.float32),
        in_specs=[vmem],
        out_specs=vmem,
        scratch_shapes=[
            pltpu.VMEM((n, 8, LANES), jnp.float32),
            pltpu.SemaphoreType.DMA((n,)),
            pltpu.SemaphoreType.DMA((n,)),
        ],
        compiler_params=pltpu.CompilerParams(collective_id=1, has_side_effects=True),
        name="rates",
    )(local)


def tally_kernel(leaf_block, recv_ref, tally_ref, sums_ref):
    sources, cells, _ = recv_ref.shape
    pairs = sources // 2
    low_half = lax.broadcasted_iota(jnp.int32, (pairs, 8, LANES), 2) < LANES // 2
    half = LANES // 2
    lo_ids = [ids16(q * 16, LANES) for q in range(half // 16)]
    hi_ids = ids16(0, LANES)
    one, zero = jnp.ones((), jnp.bfloat16), jnp.zeros((), jnp.bfloat16)

    def step(i, _):
        block = recv_ref[:, pl.ds(pl.multiple_of(i * 8, 8), 8), :]
        block = block.reshape(pairs, 2, 8, LANES)
        first, second = block[:, 0], block[:, 1]
        turned_first = pltpu.roll(first, LANES // 2, 2)
        turned_second = pltpu.roll(second, LANES // 2, 2)
        weight = jnp.where(low_half, first, turned_second)
        label = jnp.where(low_half, turned_first, second).astype(jnp.int32)
        lo = (label & (half - 1)).astype(jnp.float32)
        hi = ((label >> 7) + ((label >> 6) & 1) * 8).astype(jnp.float32)
        for j in range(8):
            a, b = [], []
            for p in range(pairs):
                low = rows16(lo[p, j:j + 1])
                a.append(jnp.where(rows16(hi[p, j:j + 1]) == hi_ids, rows16(weight[p, j:j + 1]), zero))
                b.append(jnp.concatenate([jnp.where(low == ids, one, zero) for ids in lo_ids], axis=0))
            table = nt_dot(jnp.concatenate(a, axis=1), jnp.concatenate(b, axis=1))
            tally_ref[i * 8 + j] = jnp.concatenate([table[:8], table[8:]], axis=1)
        return 0

    lax.fori_loop(0, cells // 8, step, 0)
    table = tally_ref[...]
    seen = jnp.sum(jnp.sum(table, axis=1), axis=1, keepdims=True)
    top = jnp.max(jnp.max(table, axis=1), axis=1, keepdims=True)
    tree = lax.broadcasted_iota(jnp.int32, (cells, LANES), 0) // leaf_block
    held = tree == lax.broadcasted_iota(jnp.int32, (cells, LANES), 1)
    sums_ref[...] = jnp.zeros((8, LANES), jnp.float32)
    sums_ref[0:1] = jnp.sum(jnp.where(held, seen - top, 0.0), axis=0, keepdims=True)
    sums_ref[1:2] = jnp.sum(jnp.where(held, seen, 0.0), axis=0, keepdims=True)
    sums_ref[2:3] = jnp.sum(jnp.where(held, 1.0, 0.0), axis=0, keepdims=True)


def tally(recv, leaf_block):
    sources, cells, _ = recv.shape
    high = pl.cdiv(CLASSES, LANES)
    vmem = pl.BlockSpec(memory_space=pltpu.VMEM)
    return pl.pallas_call(
        functools.partial(tally_kernel, leaf_block),
        out_shape=[
            jax.ShapeDtypeStruct((cells, high, LANES), jnp.float32),
            jax.ShapeDtypeStruct((8, LANES), jnp.float32),
        ],
        in_specs=[vmem],
        out_specs=[vmem, vmem],
        compiler_params=pltpu.CompilerParams(vmem_limit_bytes=48 << 20),
        name="tally",
    )(recv)


def per_device(leaf_index, out_of_bag, labels):
    n_rows = lax.axis_size("rows")
    tree_count = lax.axis_size("trees")
    trees = leaf_index.shape[0]
    tree_block = trees // tree_count
    leaf_block = LEAVES // n_rows
    cells = tree_block * leaf_block
    recv = compact(leaf_index, out_of_bag, labels, n_rows, tree_count)
    table, sums = tally(recv, leaf_block)
    tallies = table.reshape(cells, -1)[:, :CLASSES].reshape(tree_block, leaf_block, CLASSES)
    result = rates(sums, n_rows, tree_count)
    return tallies, result[0, :tree_block], result[1, 0]


def solution(mesh):
    in_specs = (P(None, ("rows", "trees")), P(None, ("rows", "trees")), P(("rows", "trees")))
    out_specs = (P("trees", "rows", None), P("trees"), P())
    return jax.shard_map(
        per_device, mesh=mesh, in_specs=in_specs, out_specs=out_specs, check_vma=False
    )
```

```python
import functools

import jax
import jax.numpy as jnp
from jax import lax
from jax.experimental import pallas as pl
from jax.experimental.pallas import tpu as pltpu
from jax.sharding import PartitionSpec as P

CLASSES = 1000
LEAVES = 32
LANES = 128
CHUNK = 256
GROUP = 4


def nt_dot(a, b):
    return lax.dot_general(a, b, (((1,), (1,)), ((), ())), preferred_element_type=jnp.float32)


def rows16(row):
    return jnp.broadcast_to(row, (16, row.shape[1])).astype(jnp.bfloat16)


def ids16(first, width):
    return (lax.broadcasted_iota(jnp.int32, (16, width), 0) + first).astype(jnp.float32).astype(jnp.bfloat16)


def compact_group(group, leaf_ref, weight_ref, hi_ref, lo_ref, tri_ref, mask_ref, hot_ref, placed_ref, first, slots):
    rows = leaf_ref.shape[1]
    chunks = rows // CHUNK
    one, zero = jnp.ones((), jnp.bfloat16), jnp.zeros((), jnp.bfloat16)
    leaf_ids = [ids16(q * 16, CHUNK) for q in range(LEAVES // 16)]
    slot_ids = [ids16(q * 16, CHUNK) for q in range(slots // 16)]
    leaf_ids32 = lax.broadcasted_iota(jnp.int32, (LEAVES, CHUNK), 0)
    for j in range(group):
        for c in range(chunks):
            cols = slice(c * CHUNK, (c + 1) * CHUNK)
            leaf = rows16(leaf_ref[pl.ds(first + j, 1), cols].astype(jnp.float32))
            weight = rows16(weight_ref[pl.ds(first + j, 1), cols])
            for q in range(LEAVES // 16):
                mask = leaf == leaf_ids[q]
                at = (j * chunks + c) * LEAVES + q * 16
                mask_ref[at:at + 16, :] = jnp.where(mask, one, zero)
                at = j * 3 * LEAVES + q * 16
                placed_ref[at:at + 16, cols] = jnp.where(mask, weight, zero)
                placed_ref[at + LEAVES:at + LEAVES + 16, cols] = jnp.where(mask, hi_ref[:, cols], zero)
                placed_ref[at + 2 * LEAVES:at + 2 * LEAVES + 16, cols] = jnp.where(mask, lo_ref[:, cols], zero)
    counts = jnp.dot(mask_ref[...], tri_ref[...], preferred_element_type=jnp.float32)
    for j in range(group):
        carry = jnp.zeros((LEAVES, 1), jnp.float32)
        for c in range(chunks):
            cols = slice(c * CHUNK, (c + 1) * CHUNK)
            at = (j * chunks + c) * LEAVES
            running = counts[at:at + LEAVES] + carry
            carry = running[:, CHUNK - 1:]
            mask = leaf_ref[pl.ds(first + j, 1), cols] == leaf_ids32
            rank = rows16(jnp.sum(jnp.where(mask, running, 0.0), axis=0, keepdims=True) - 1.0)
            for q in range(slots // 16):
                at = j * slots + q * 16
                hot_ref[at:at + 16, cols] = jnp.where(rank == slot_ids[q], one, zero)
    out = nt_dot(placed_ref[...], hot_ref[...])
    parts = []
    for j in range(group):
        mine = out[j * 3 * LEAVES:(j + 1) * 3 * LEAVES, j * slots:(j + 1) * slots]
        classes = mine[LEAVES:2 * LEAVES] + mine[2 * LEAVES:]
        parts.append(jnp.concatenate([mine[:LEAVES], classes], axis=1))
    return parts


def others(n, me, body):
    lax.fori_loop(1, n, lambda k, _: body(lax.rem(me + k, n)) or 0, 0)


def greet_all(n, tree_count, me):
    barrier = pltpu.get_barrier_semaphore()

    def greet(other):
        pl.semaphore_signal(
            barrier, inc=1, device_id=(other // tree_count, lax.rem(other, tree_count)),
            device_id_type=pl.DeviceIdType.MESH,
        )

    others(n, me, greet)
    return lambda: pl.semaphore_wait(barrier, n - 1)


def add_batch(recv_ref, tally_ref, index_of, sources):
    cells = recv_ref.shape[1]
    pairs = sources // 2
    half = LANES // 2
    low_half = lax.broadcasted_iota(jnp.int32, (8, LANES), 1) < half
    lo_ids = [ids16(q * 16, LANES) for q in range(half // 16)]
    hi_ids = ids16(0, LANES)
    one, zero = jnp.ones((), jnp.bfloat16), jnp.zeros((), jnp.bfloat16)

    def step(i, _):
        at = pl.ds(pl.multiple_of(i * 8, 8), 8)
        weights, los, his = [], [], []
        for p in range(pairs):
            first, second = recv_ref[index_of(2 * p), at, :], recv_ref[index_of(2 * p + 1), at, :]
            weights.append(jnp.where(low_half, first, pltpu.roll(second, half, 1)))
            label = jnp.where(low_half, pltpu.roll(first, half, 1), second).astype(jnp.int32)
            los.append((label & (half - 1)).astype(jnp.float32))
            his.append(((label >> 7) + ((label >> 6) & 1) * 8).astype(jnp.float32))
        for j in range(8):
            a, b = [], []
            for p in range(pairs):
                low = rows16(los[p][j:j + 1])
                a.append(jnp.where(rows16(his[p][j:j + 1]) == hi_ids, rows16(weights[p][j:j + 1]), zero))
                b.append(jnp.concatenate([jnp.where(low == ids, one, zero) for ids in lo_ids], axis=0))
            table = nt_dot(jnp.concatenate(a, axis=1), jnp.concatenate(b, axis=1))
            tally_ref[i * 8 + j] += jnp.concatenate([table[:8], table[8:]], axis=1)
        return 0

    lax.fori_loop(0, cells // 8, step, 0)


def forest_kernel(n_rows, tree_count, leaf_ref, bag_ref, label_ref, tally_ref, tree_ref, forest_ref,
                  send_ref, recv_ref, sums_ref, all_sums_ref, weight_ref, hi_ref, lo_ref, tri_ref,
                  mask_a, hot_a, placed_a, mask_b, hot_b, placed_b,
                  send_sem, recv_sem, own_sem, sums_send_sem, sums_recv_sem):
    trees, rows = leaf_ref.shape
    slots = rows // LEAVES
    leaf_block = LEAVES // n_rows
    tree_block = trees // tree_count
    cells = tree_block * leaf_block
    size = 2 * GROUP * leaf_block
    n = n_rows * tree_count
    my_row, my_tree = lax.axis_index("rows"), lax.axis_index("trees")
    me = my_row * tree_count + my_tree
    wait_all = greet_all(n, tree_count, me)

    labels = label_ref[...]
    hi = (labels >> 5) << 5
    hi_ref[...] = rows16(hi.astype(jnp.float32))
    lo_ref[...] = rows16((labels - hi).astype(jnp.float32))
    r = lax.broadcasted_iota(jnp.int32, (CHUNK, CHUNK), 0)
    c = lax.broadcasted_iota(jnp.int32, (CHUNK, CHUNK), 1)
    tri_ref[...] = jnp.where(r <= c, 1.0, 0.0).astype(jnp.bfloat16)
    weight_ref[...] = bag_ref[...].astype(jnp.float32)
    tally_ref[...] = jnp.zeros_like(tally_ref)
    wait_all()

    def remote(src, dst, sender, receiver, other):
        return pltpu.make_async_remote_copy(
            src_ref=src, dst_ref=dst, send_sem=sender, recv_sem=receiver,
            device_id=(other // tree_count, lax.rem(other, tree_count)),
            device_id_type=pl.DeviceIdType.MESH,
        )

    def piece(i, tt):
        first = tt * tree_block + i * 2 * GROUP
        parts = compact_group(GROUP, leaf_ref, weight_ref, hi_ref, lo_ref, tri_ref,
                              mask_a, hot_a, placed_a, first, slots)
        parts += compact_group(GROUP, leaf_ref, weight_ref, hi_ref, lo_ref, tri_ref,
                               mask_b, hot_b, placed_b, first + GROUP, slots)
        at = pl.ds(pl.multiple_of(i * size, size), size)
        for b in range(n_rows):
            tile = jnp.concatenate([p[b * leaf_block:(b + 1) * leaf_block] for p in parts], axis=0)
            send_ref[b * tree_count + tt, at, :] = tile

        def send(k, _):
            other = lax.rem(my_row + k, n_rows) * tree_count + tt

            @pl.when(other != me)
            def _():
                remote(send_ref.at[other, at], recv_ref.at[me, at], send_sem.at[other], recv_sem.at[me], other).start()

            return 0

        lax.fori_loop(0, n_rows, send, 0)

    def whole(other):
        return remote(send_ref.at[other], recv_ref.at[other], send_sem.at[other], recv_sem.at[other], other)

    own = pltpu.make_async_copy(send_ref.at[me], recv_ref.at[me], own_sem)

    def phase(i, _):
        @pl.when(i < tree_count)
        def _():
            tt = lax.rem(my_tree + i + 1, tree_count)
            lax.fori_loop(0, tree_block // (2 * GROUP), lambda j, _: piece(j, tt) or 0, 0)

        @pl.when(i == tree_count - 1)
        def _():
            own.start()

        @pl.when(i > 0)
        def _():
            sender = lax.rem(my_tree + tree_count - i, tree_count)

            def arrive(row, _):
                other = row * tree_count + sender
                pl.when(other != me)(lambda: whole(other).wait_recv())
                return 0

            lax.fori_loop(0, n_rows, arrive, 0)
            pl.when(i == tree_count)(own.wait)
            add_batch(recv_ref, tally_ref, lambda row: row * tree_count + sender, n_rows)

        return 0

    lax.fori_loop(0, tree_count + 1, phase, 0)

    table = tally_ref[...]
    seen = jnp.sum(jnp.sum(table, axis=1), axis=1, keepdims=True)
    top = jnp.max(jnp.max(table, axis=1), axis=1, keepdims=True)
    tree = lax.broadcasted_iota(jnp.int32, (cells, LANES), 0) // leaf_block
    held = tree == lax.broadcasted_iota(jnp.int32, (cells, LANES), 1)
    sums_ref[...] = jnp.zeros((8, LANES), jnp.float32)
    sums_ref[0:1] = jnp.sum(jnp.where(held, seen - top, 0.0), axis=0, keepdims=True)
    sums_ref[1:2] = jnp.sum(jnp.where(held, seen, 0.0), axis=0, keepdims=True)

    def sums_copy(slot, other):
        return remote(sums_ref, all_sums_ref.at[slot], sums_send_sem.at[other], sums_recv_sem.at[slot], other)

    others(n, me, lambda other: sums_copy(me, other).start())
    all_sums_ref[me] = sums_ref[...]
    others(n, me, lambda other: whole(other).wait_send())
    others(n, me, lambda other: sums_copy(other, other).wait())
    mine = jnp.zeros((8, LANES), jnp.float32)
    total = jnp.zeros((8, LANES), jnp.float32)
    for row in range(n_rows):
        mine += all_sums_ref[row * tree_count + my_tree]
    for device in range(n):
        total += all_sums_ref[device]
    pooled = jnp.sum(total, axis=1, keepdims=True)
    tree_ref[...] = mine[0:1, :tree_block] / mine[1:2, :tree_block]
    forest_ref[...] = pooled[0:1] / pooled[1:2]


def forest(leaf_index, out_of_bag, labels, n_rows, tree_count):
    trees, rows = leaf_index.shape
    n = n_rows * tree_count
    tree_block = trees // tree_count
    cells = tree_block * (LEAVES // n_rows)
    vmem = pl.BlockSpec(memory_space=pltpu.VMEM)
    group_scratch = [
        pltpu.VMEM((GROUP * LEAVES * (rows // CHUNK), CHUNK), jnp.bfloat16),
        pltpu.VMEM((GROUP * (rows // LEAVES), rows), jnp.bfloat16),
        pltpu.VMEM((GROUP * 3 * LEAVES, rows), jnp.bfloat16),
    ]
    return pl.pallas_call(
        functools.partial(forest_kernel, n_rows, tree_count),
        out_shape=[
            jax.ShapeDtypeStruct((cells, pl.cdiv(CLASSES, LANES), LANES), jnp.float32),
            jax.ShapeDtypeStruct((1, tree_block), jnp.float32),
            jax.ShapeDtypeStruct((1, 1), jnp.float32),
        ],
        in_specs=[vmem] * 3,
        out_specs=[vmem] * 3,
        scratch_shapes=[
            pltpu.VMEM((n, cells, LANES), jnp.float32),
            pltpu.VMEM((n, cells, LANES), jnp.float32),
            pltpu.VMEM((8, LANES), jnp.float32),
            pltpu.VMEM((n, 8, LANES), jnp.float32),
            pltpu.VMEM((trees, rows), jnp.float32),
            pltpu.VMEM((16, rows), jnp.bfloat16),
            pltpu.VMEM((16, rows), jnp.bfloat16),
            pltpu.VMEM((CHUNK, CHUNK), jnp.bfloat16),
            *group_scratch,
            *group_scratch,
            pltpu.SemaphoreType.DMA((n,)),
            pltpu.SemaphoreType.DMA((n,)),
            pltpu.SemaphoreType.DMA,
            pltpu.SemaphoreType.DMA((n,)),
            pltpu.SemaphoreType.DMA((n,)),
        ],
        compiler_params=pltpu.CompilerParams(
            vmem_limit_bytes=48 << 20, collective_id=0, has_side_effects=True
        ),
        name="forest",
    )(leaf_index, out_of_bag, labels.reshape(1, rows))


def per_device(leaf_index, out_of_bag, labels):
    n_rows = lax.axis_size("rows")
    tree_count = lax.axis_size("trees")
    trees = leaf_index.shape[0]
    tree_block = trees // tree_count
    leaf_block = LEAVES // n_rows
    cells = tree_block * leaf_block
    table, tree_error, pooled = forest(leaf_index, out_of_bag, labels, n_rows, tree_count)
    tallies = table.reshape(cells, -1)[:, :CLASSES].reshape(tree_block, leaf_block, CLASSES)
    return tallies, tree_error.reshape(tree_block), pooled.reshape(())


def solution(mesh):
    in_specs = (P(None, ("rows", "trees")), P(None, ("rows", "trees")), P(("rows", "trees")))
    out_specs = (P("trees", "rows", None), P("trees"), P())
    return jax.shard_map(
        per_device, mesh=mesh, in_specs=in_specs, out_specs=out_specs, check_vma=False
    )
```

```python
import functools

import jax
import jax.numpy as jnp
from jax import lax
from jax.experimental import pallas as pl
from jax.experimental.pallas import tpu as pltpu
from jax.sharding import PartitionSpec as P

CLASSES = 1000
LEAVES = 32
LANES = 128
CHUNK = 256
GROUP = 4
COUNT_STEP = 128.0


def nt_dot(a, b):
    return lax.dot_general(a, b, (((1,), (1,)), ((), ())), preferred_element_type=jnp.float32)


def rows16(row):
    return jnp.broadcast_to(row, (16, row.shape[1])).astype(jnp.bfloat16)


def ids16(first, width):
    return (lax.broadcasted_iota(jnp.int32, (16, width), 0) + first).astype(jnp.float32).astype(jnp.bfloat16)


def compact_group(group, leaf_ref, weight_ref, code_ref, tri_ref, mask_ref, hot_ref, placed_ref, first, slots):
    rows = leaf_ref.shape[1]
    chunks = rows // CHUNK
    one, zero = jnp.ones((), jnp.bfloat16), jnp.zeros((), jnp.bfloat16)
    second = jnp.full((), COUNT_STEP, jnp.bfloat16)
    leaf_ids = [ids16(q * 16, CHUNK) for q in range(LEAVES // 16)]
    slot_ids = [ids16(q * 16, CHUNK) for q in range(slots // 16)]
    leaf_ids32 = lax.broadcasted_iota(jnp.int32, (LEAVES, CHUNK), 0)
    for pair in range(group // 2):
        for c in range(chunks):
            cols = slice(c * CHUNK, (c + 1) * CHUNK)
            code = code_ref[:, cols]
            masks = []
            for j in (2 * pair, 2 * pair + 1):
                leaf = rows16(leaf_ref[pl.ds(first + j, 1), cols].astype(jnp.float32))
                weight = rows16(weight_ref[pl.ds(first + j, 1), cols])
                masks.append([leaf == ids for ids in leaf_ids])
                for q, mask in enumerate(masks[-1]):
                    at = j * 2 * LEAVES + q * 16
                    placed_ref[at:at + 16, cols] = jnp.where(mask, weight, zero)
                    placed_ref[at + LEAVES:at + LEAVES + 16, cols] = jnp.where(mask, code, zero)
            for q in range(LEAVES // 16):
                at = (pair * chunks + c) * LEAVES + q * 16
                mask_ref[at:at + 16, :] = jnp.where(masks[0][q], one, zero) + jnp.where(masks[1][q], second, zero)
    counts = jnp.dot(mask_ref[...], tri_ref[...], preferred_element_type=jnp.float32)
    for pair in range(group // 2):
        carry = jnp.zeros((LEAVES, 1), jnp.float32)
        for c in range(chunks):
            cols = slice(c * CHUNK, (c + 1) * CHUNK)
            at = (pair * chunks + c) * LEAVES
            running = counts[at:at + LEAVES] + carry
            carry = running[:, CHUNK - 1:]
            for side in range(2):
                j = 2 * pair + side
                mask = leaf_ref[pl.ds(first + j, 1), cols] == leaf_ids32
                both = jnp.sum(jnp.where(mask, running, 0.0), axis=0, keepdims=True)
                high = jnp.floor(both * (1.0 / COUNT_STEP))
                rank = rows16((high if side else both - high * COUNT_STEP) - 1.0)
                for q in range(slots // 16):
                    at_slot = j * slots + q * 16
                    hot_ref[at_slot:at_slot + 16, cols] = jnp.where(rank == slot_ids[q], one, zero)
    out = nt_dot(placed_ref[...], hot_ref[...])
    parts = []
    for j in range(group):
        mine = out[j * 2 * LEAVES:(j + 1) * 2 * LEAVES, j * slots:(j + 1) * slots]
        parts.append(jnp.concatenate([mine[:LEAVES], mine[LEAVES:]], axis=1))
    return parts


def others(n, me, body):
    lax.fori_loop(1, n, lambda k, _: body(lax.rem(me + k, n)) or 0, 0)


def greet_all(n, tree_count, me):
    barrier = pltpu.get_barrier_semaphore()

    def greet(other):
        pl.semaphore_signal(
            barrier, inc=1, device_id=(other // tree_count, lax.rem(other, tree_count)),
            device_id_type=pl.DeviceIdType.MESH,
        )

    others(n, me, greet)
    return lambda: pl.semaphore_wait(barrier, n - 1)


def add_batch(recv_ref, tally_ref, index_of, sources):
    cells = recv_ref.shape[1]
    pairs = sources // 2
    half = LANES // 2
    low_half = lax.broadcasted_iota(jnp.int32, (8, LANES), 1) < half
    lo_ids = [ids16(q * 16, LANES) for q in range(half // 16)]
    hi_ids = ids16(0, LANES)
    one, zero = jnp.ones((), jnp.bfloat16), jnp.zeros((), jnp.bfloat16)

    def step(i, _):
        at = pl.ds(pl.multiple_of(i * 8, 8), 8)
        weights, los, his = [], [], []
        for p in range(pairs):
            first, second = recv_ref[index_of(2 * p), at, :], recv_ref[index_of(2 * p + 1), at, :]
            weights.append(jnp.where(low_half, first, pltpu.roll(second, half, 1)))
            code = jnp.where(low_half, pltpu.roll(first, half, 1), second)
            power = jnp.zeros((8, LANES), jnp.int32)
            for k in range(1, -(-CLASSES // LANES)):
                power += jnp.where(code >= float(LANES << k), 1, 0)
            low = (code.astype(jnp.int32) >> power) & (LANES - 1)
            los.append((low & (half - 1)).astype(jnp.float32))
            his.append((power + (low >> 6) * 8).astype(jnp.float32))
        for j in range(8):
            a, b = [], []
            for p in range(pairs):
                low = rows16(los[p][j:j + 1])
                a.append(jnp.where(rows16(his[p][j:j + 1]) == hi_ids, rows16(weights[p][j:j + 1]), zero))
                b.append(jnp.concatenate([jnp.where(low == ids, one, zero) for ids in lo_ids], axis=0))
            table = nt_dot(jnp.concatenate(a, axis=1), jnp.concatenate(b, axis=1))
            tally_ref[i * 8 + j] += jnp.concatenate([table[:8], table[8:]], axis=1)
        return 0

    lax.fori_loop(0, cells // 8, step, 0)


def forest_kernel(n_rows, tree_count, leaf_ref, bag_ref, label_ref, tally_ref, tree_ref, forest_ref,
                  send_ref, recv_ref, sums_ref, all_sums_ref, weight_ref, code_ref, tri_ref,
                  mask_a, hot_a, placed_a, mask_b, hot_b, placed_b,
                  send_sem, recv_sem, own_sem, sums_send_sem, sums_recv_sem):
    trees, rows = leaf_ref.shape
    slots = rows // LEAVES
    leaf_block = LEAVES // n_rows
    tree_block = trees // tree_count
    cells = tree_block * leaf_block
    size = 2 * GROUP * leaf_block
    n = n_rows * tree_count
    my_row, my_tree = lax.axis_index("rows"), lax.axis_index("trees")
    me = my_row * tree_count + my_tree
    wait_all = greet_all(n, tree_count, me)

    labels = label_ref[...]
    code_ref[...] = rows16(((labels % LANES + LANES) << (labels // LANES)).astype(jnp.float32))
    r = lax.broadcasted_iota(jnp.int32, (CHUNK, CHUNK), 0)
    c = lax.broadcasted_iota(jnp.int32, (CHUNK, CHUNK), 1)
    tri_ref[...] = jnp.where(r <= c, 1.0, 0.0).astype(jnp.bfloat16)
    weight_ref[...] = bag_ref[...].astype(jnp.float32)
    tally_ref[...] = jnp.zeros_like(tally_ref)
    wait_all()

    def remote(src, dst, sender, receiver, other):
        return pltpu.make_async_remote_copy(
            src_ref=src, dst_ref=dst, send_sem=sender, recv_sem=receiver,
            device_id=(other // tree_count, lax.rem(other, tree_count)),
            device_id_type=pl.DeviceIdType.MESH,
        )

    def piece(i, tt):
        first = tt * tree_block + i * 2 * GROUP
        parts = compact_group(GROUP, leaf_ref, weight_ref, code_ref, tri_ref,
                              mask_a, hot_a, placed_a, first, slots)
        parts += compact_group(GROUP, leaf_ref, weight_ref, code_ref, tri_ref,
                               mask_b, hot_b, placed_b, first + GROUP, slots)
        at = pl.ds(pl.multiple_of(i * size, size), size)
        for b in range(n_rows):
            tile = jnp.concatenate([p[b * leaf_block:(b + 1) * leaf_block] for p in parts], axis=0)
            send_ref[b * tree_count + tt, at, :] = tile

        def send(k, _):
            other = lax.rem(my_row + k, n_rows) * tree_count + tt

            @pl.when(other != me)
            def _():
                remote(send_ref.at[other, at], recv_ref.at[me, at], send_sem.at[other], recv_sem.at[me], other).start()

            return 0

        lax.fori_loop(0, n_rows, send, 0)

    def whole(other):
        return remote(send_ref.at[other], recv_ref.at[other], send_sem.at[other], recv_sem.at[other], other)

    own = pltpu.make_async_copy(send_ref.at[me], recv_ref.at[me], own_sem)

    def phase(i, _):
        @pl.when(i < tree_count)
        def _():
            tt = lax.rem(my_tree + i + 1, tree_count)
            lax.fori_loop(0, tree_block // (2 * GROUP), lambda j, _: piece(j, tt) or 0, 0)

        @pl.when(i == tree_count - 1)
        def _():
            own.start()

        @pl.when(i > 0)
        def _():
            sender = lax.rem(my_tree + tree_count - i, tree_count)

            def arrive(row, _):
                other = row * tree_count + sender
                pl.when(other != me)(lambda: whole(other).wait_recv())
                return 0

            lax.fori_loop(0, n_rows, arrive, 0)
            pl.when(i == tree_count)(own.wait)
            add_batch(recv_ref, tally_ref, lambda row: row * tree_count + sender, n_rows)

        return 0

    lax.fori_loop(0, tree_count + 1, phase, 0)

    table = tally_ref[...]
    seen = jnp.sum(jnp.sum(table, axis=1), axis=1, keepdims=True)
    top = jnp.max(jnp.max(table, axis=1), axis=1, keepdims=True)
    tree = lax.broadcasted_iota(jnp.int32, (cells, LANES), 0) // leaf_block
    held = tree == lax.broadcasted_iota(jnp.int32, (cells, LANES), 1)
    sums_ref[...] = jnp.zeros((8, LANES), jnp.float32)
    sums_ref[0:1] = jnp.sum(jnp.where(held, seen - top, 0.0), axis=0, keepdims=True)
    sums_ref[1:2] = jnp.sum(jnp.where(held, seen, 0.0), axis=0, keepdims=True)

    def sums_copy(slot, other):
        return remote(sums_ref, all_sums_ref.at[slot], sums_send_sem.at[other], sums_recv_sem.at[slot], other)

    others(n, me, lambda other: sums_copy(me, other).start())
    all_sums_ref[me] = sums_ref[...]
    others(n, me, lambda other: whole(other).wait_send())
    others(n, me, lambda other: sums_copy(other, other).wait())
    mine = jnp.zeros((8, LANES), jnp.float32)
    total = jnp.zeros((8, LANES), jnp.float32)
    for row in range(n_rows):
        mine += all_sums_ref[row * tree_count + my_tree]
    for device in range(n):
        total += all_sums_ref[device]
    pooled = jnp.sum(total, axis=1, keepdims=True)
    tree_ref[...] = mine[0:1, :tree_block] / mine[1:2, :tree_block]
    forest_ref[...] = pooled[0:1] / pooled[1:2]


def forest(leaf_index, out_of_bag, labels, n_rows, tree_count):
    trees, rows = leaf_index.shape
    n = n_rows * tree_count
    tree_block = trees // tree_count
    cells = tree_block * (LEAVES // n_rows)
    vmem = pl.BlockSpec(memory_space=pltpu.VMEM)
    group_scratch = [
        pltpu.VMEM((GROUP // 2 * LEAVES * (rows // CHUNK), CHUNK), jnp.bfloat16),
        pltpu.VMEM((GROUP * (rows // LEAVES), rows), jnp.bfloat16),
        pltpu.VMEM((GROUP * 2 * LEAVES, rows), jnp.bfloat16),
    ]
    return pl.pallas_call(
        functools.partial(forest_kernel, n_rows, tree_count),
        out_shape=[
            jax.ShapeDtypeStruct((cells, pl.cdiv(CLASSES, LANES), LANES), jnp.float32),
            jax.ShapeDtypeStruct((1, tree_block), jnp.float32),
            jax.ShapeDtypeStruct((1, 1), jnp.float32),
        ],
        in_specs=[vmem] * 3,
        out_specs=[vmem] * 3,
        scratch_shapes=[
            pltpu.VMEM((n, cells, LANES), jnp.float32),
            pltpu.VMEM((n, cells, LANES), jnp.float32),
            pltpu.VMEM((8, LANES), jnp.float32),
            pltpu.VMEM((n, 8, LANES), jnp.float32),
            pltpu.VMEM((trees, rows), jnp.float32),
            pltpu.VMEM((16, rows), jnp.bfloat16),
            pltpu.VMEM((CHUNK, CHUNK), jnp.bfloat16),
            *group_scratch,
            *group_scratch,
            pltpu.SemaphoreType.DMA((n,)),
            pltpu.SemaphoreType.DMA((n,)),
            pltpu.SemaphoreType.DMA,
            pltpu.SemaphoreType.DMA((n,)),
            pltpu.SemaphoreType.DMA((n,)),
        ],
        compiler_params=pltpu.CompilerParams(
            vmem_limit_bytes=48 << 20, collective_id=0, has_side_effects=True
        ),
        name="forest",
    )(leaf_index, out_of_bag, labels.reshape(1, rows))


def per_device(leaf_index, out_of_bag, labels):
    n_rows = lax.axis_size("rows")
    tree_count = lax.axis_size("trees")
    trees = leaf_index.shape[0]
    tree_block = trees // tree_count
    leaf_block = LEAVES // n_rows
    cells = tree_block * leaf_block
    table, tree_error, pooled = forest(leaf_index, out_of_bag, labels, n_rows, tree_count)
    tallies = table.reshape(cells, -1)[:, :CLASSES].reshape(tree_block, leaf_block, CLASSES)
    return tallies, tree_error.reshape(tree_block), pooled.reshape(())


def solution(mesh):
    in_specs = (P(None, ("rows", "trees")), P(None, ("rows", "trees")), P(("rows", "trees")))
    out_specs = (P("trees", "rows", None), P("trees"), P())
    return jax.shard_map(
        per_device, mesh=mesh, in_specs=in_specs, out_specs=out_specs, check_vma=False
    )
```

```python
import functools

import jax
import jax.numpy as jnp
from jax import lax
from jax.experimental import pallas as pl
from jax.experimental.pallas import tpu as pltpu
from jax.sharding import PartitionSpec as P

CLASSES = 1000
LEAVES = 32
LANES = 128
CHUNK = 256
GROUP = 8
BATCH = 4
COUNT_STEP = 128.0


def nt_dot(a, b):
    return lax.dot_general(a, b, (((1,), (1,)), ((), ())), preferred_element_type=jnp.float32)


def rows16(row):
    return jnp.broadcast_to(row, (16, row.shape[1])).astype(jnp.bfloat16)


def ids16(first, width):
    return (lax.broadcasted_iota(jnp.int32, (16, width), 0) + first).astype(jnp.float32).astype(jnp.bfloat16)


def compact_group(group, leaf_ref, weight_ref, code_ref, tri_ref, mask_ref, hot_ref, placed_ref, first, slots):
    rows = leaf_ref.shape[1]
    chunks = rows // CHUNK
    one, zero = jnp.ones((), jnp.bfloat16), jnp.zeros((), jnp.bfloat16)
    second = jnp.full((), COUNT_STEP, jnp.bfloat16)
    leaf_ids = [ids16(q * 16, CHUNK) for q in range(LEAVES // 16)]
    slot_ids = [ids16(q * 16, CHUNK) for q in range(slots // 16)]
    leaf_ids32 = lax.broadcasted_iota(jnp.int32, (LEAVES, CHUNK), 0)
    for pair in range(group // 2):
        for c in range(chunks):
            cols = slice(c * CHUNK, (c + 1) * CHUNK)
            code = code_ref[:, cols]
            masks = []
            for j in (2 * pair, 2 * pair + 1):
                leaf = rows16(leaf_ref[pl.ds(first + j, 1), cols].astype(jnp.float32))
                weight = rows16(weight_ref[pl.ds(first + j, 1), cols])
                masks.append([leaf == ids for ids in leaf_ids])
                for q, mask in enumerate(masks[-1]):
                    at = j * 2 * LEAVES + q * 16
                    placed_ref[at:at + 16, cols] = jnp.where(mask, weight, zero)
                    placed_ref[at + LEAVES:at + LEAVES + 16, cols] = jnp.where(mask, code, zero)
            for q in range(LEAVES // 16):
                at = (pair * chunks + c) * LEAVES + q * 16
                mask_ref[at:at + 16, :] = jnp.where(masks[0][q], one, zero) + jnp.where(masks[1][q], second, zero)
    counts = jnp.dot(mask_ref[...], tri_ref[...], preferred_element_type=jnp.float32)
    for pair in range(group // 2):
        carry = jnp.zeros((LEAVES, LANES), jnp.float32)
        for c in range(chunks):
            cols = slice(c * CHUNK, (c + 1) * CHUNK)
            at = (pair * chunks + c) * LEAVES
            here = counts[at:at + LEAVES]
            running = here + jnp.concatenate([carry] * (CHUNK // LANES), axis=1)
            carry = carry + jnp.broadcast_to(here[:, CHUNK - 1:], (LEAVES, LANES))
            for side in range(2):
                j = 2 * pair + side
                mask = leaf_ref[pl.ds(first + j, 1), cols] == leaf_ids32
                both = jnp.sum(jnp.where(mask, running, 0.0), axis=0, keepdims=True)
                high = jnp.floor(both * (1.0 / COUNT_STEP))
                rank = rows16((high if side else both - high * COUNT_STEP) - 1.0)
                for q in range(slots // 16):
                    at_slot = j * slots + q * 16
                    hot_ref[at_slot:at_slot + 16, cols] = jnp.where(rank == slot_ids[q], one, zero)
    parts = []
    for base in range(0, group, BATCH):
        out = nt_dot(placed_ref[base * 2 * LEAVES:(base + BATCH) * 2 * LEAVES, :],
                     hot_ref[base * slots:(base + BATCH) * slots, :])
        for j in range(BATCH):
            mine = out[j * 2 * LEAVES:(j + 1) * 2 * LEAVES, j * slots:(j + 1) * slots]
            parts.append(jnp.concatenate([mine[:LEAVES], mine[LEAVES:]], axis=1))
    return parts


def others(n, me, body):
    lax.fori_loop(1, n, lambda k, _: body(lax.rem(me + k, n)) or 0, 0)


def greet_all(n, tree_count, me):
    barrier = pltpu.get_barrier_semaphore()

    def greet(other):
        pl.semaphore_signal(
            barrier, inc=1, device_id=(other // tree_count, lax.rem(other, tree_count)),
            device_id_type=pl.DeviceIdType.MESH,
        )

    others(n, me, greet)
    return lambda: pl.semaphore_wait(barrier, n - 1)


def add_batch(recv_ref, tally_ref, index_of, sources):
    cells = recv_ref.shape[1]
    pairs = sources // 2
    half = LANES // 2
    low_half = lax.broadcasted_iota(jnp.int32, (8, LANES), 1) < half
    lo_ids = [ids16(q * 16, LANES) for q in range(half // 16)]
    hi_ids = ids16(0, LANES)
    one, zero = jnp.ones((), jnp.bfloat16), jnp.zeros((), jnp.bfloat16)

    def step(i, _):
        at = pl.ds(pl.multiple_of(i * 8, 8), 8)
        weights, los, his = [], [], []
        for p in range(pairs):
            first, second = recv_ref[index_of(2 * p), at, :], recv_ref[index_of(2 * p + 1), at, :]
            weights.append(jnp.where(low_half, first, pltpu.roll(second, half, 1)))
            code = jnp.where(low_half, pltpu.roll(first, half, 1), second)
            power = jnp.zeros((8, LANES), jnp.int32)
            for k in range(1, -(-CLASSES // LANES)):
                power += jnp.where(code >= float(LANES << k), 1, 0)
            low = (code.astype(jnp.int32) >> power) & (LANES - 1)
            los.append((low & (half - 1)).astype(jnp.float32))
            his.append((power + (low >> 6) * 8).astype(jnp.float32))
        for j in range(8):
            a, b = [], []
            for p in range(pairs):
                low = rows16(los[p][j:j + 1])
                a.append(jnp.where(rows16(his[p][j:j + 1]) == hi_ids, rows16(weights[p][j:j + 1]), zero))
                b.append(jnp.concatenate([jnp.where(low == ids, one, zero) for ids in lo_ids], axis=0))
            table = nt_dot(jnp.concatenate(a, axis=1), jnp.concatenate(b, axis=1))
            tally_ref[i * 8 + j] += jnp.concatenate([table[:8], table[8:]], axis=1)
        return 0

    lax.fori_loop(0, cells // 8, step, 0)


def forest_kernel(n_rows, tree_count, leaf_in, bag_in, label_in, tally_ref, tree_ref, forest_ref,
                  send_ref, recv_ref, sums_ref, all_sums_ref, weight_ref, code_ref, tri_ref,
                  mask_ref, hot_ref, placed_ref, leaf_ref, bag_ref, label_ref, in_sem,
                  send_sem, recv_sem, own_sem, sums_send_sem, sums_recv_sem):
    trees, rows = leaf_ref.shape
    slots = rows // LEAVES
    leaf_block = LEAVES // n_rows
    tree_block = trees // tree_count
    cells = tree_block * leaf_block
    size = GROUP * leaf_block
    n = n_rows * tree_count
    my_row, my_tree = lax.axis_index("rows"), lax.axis_index("trees")
    me = my_row * tree_count + my_tree
    loads = [
        pltpu.make_async_copy(src, dst, in_sem.at[k])
        for k, (src, dst) in enumerate([(leaf_in, leaf_ref), (bag_in, bag_ref), (label_in, label_ref)])
    ]
    for load in loads:
        load.start()
    wait_all = greet_all(n, tree_count, me)
    tally_ref[...] = jnp.zeros_like(tally_ref)
    for load in loads:
        load.wait()

    labels = label_ref[...]
    code_ref[...] = rows16(((labels % LANES + LANES) << (labels // LANES)).astype(jnp.float32))
    r = lax.broadcasted_iota(jnp.int32, (CHUNK, CHUNK), 0)
    c = lax.broadcasted_iota(jnp.int32, (CHUNK, CHUNK), 1)
    tri_ref[...] = jnp.where(r <= c, 1.0, 0.0).astype(jnp.bfloat16)
    weight_ref[...] = bag_ref[...].astype(jnp.float32)
    wait_all()

    def remote(src, dst, sender, receiver, other):
        return pltpu.make_async_remote_copy(
            src_ref=src, dst_ref=dst, send_sem=sender, recv_sem=receiver,
            device_id=(other // tree_count, lax.rem(other, tree_count)),
            device_id_type=pl.DeviceIdType.MESH,
        )

    def piece(i, tt):
        first = tt * tree_block + i * GROUP
        parts = compact_group(GROUP, leaf_ref, weight_ref, code_ref, tri_ref,
                              mask_ref, hot_ref, placed_ref, first, slots)
        at = pl.ds(pl.multiple_of(i * size, size), size)
        for b in range(n_rows):
            tile = jnp.concatenate([p[b * leaf_block:(b + 1) * leaf_block] for p in parts], axis=0)
            send_ref[b * tree_count + tt, at, :] = tile

        def send(k, _):
            other = lax.rem(my_row + k, n_rows) * tree_count + tt

            @pl.when(other != me)
            def _():
                remote(send_ref.at[other, at], recv_ref.at[me, at], send_sem.at[other], recv_sem.at[me], other).start()

            return 0

        lax.fori_loop(0, n_rows, send, 0)

    def whole(other):
        return remote(send_ref.at[other], recv_ref.at[other], send_sem.at[other], recv_sem.at[other], other)

    own = pltpu.make_async_copy(send_ref.at[me], recv_ref.at[me], own_sem)

    def phase(i, _):
        @pl.when(i < tree_count)
        def _():
            tt = lax.rem(my_tree + i + 1, tree_count)
            lax.fori_loop(0, tree_block // GROUP, lambda j, _: piece(j, tt) or 0, 0)

        @pl.when(i == tree_count - 1)
        def _():
            own.start()

        @pl.when(i > 0)
        def _():
            sender = lax.rem(my_tree + tree_count - i, tree_count)

            def arrive(row, _):
                other = row * tree_count + sender
                pl.when(other != me)(lambda: whole(other).wait_recv())
                return 0

            lax.fori_loop(0, n_rows, arrive, 0)
            pl.when(i == tree_count)(own.wait)
            add_batch(recv_ref, tally_ref, lambda row: row * tree_count + sender, n_rows)

        return 0

    lax.fori_loop(0, tree_count + 1, phase, 0)

    table = tally_ref[...]
    seen = jnp.sum(jnp.sum(table, axis=1), axis=1, keepdims=True)
    top = jnp.max(jnp.max(table, axis=1), axis=1, keepdims=True)
    tree = lax.broadcasted_iota(jnp.int32, (cells, LANES), 0) // leaf_block
    held = tree == lax.broadcasted_iota(jnp.int32, (cells, LANES), 1)
    sums_ref[...] = jnp.zeros((8, LANES), jnp.float32)
    sums_ref[0:1] = jnp.sum(jnp.where(held, seen - top, 0.0), axis=0, keepdims=True)
    sums_ref[1:2] = jnp.sum(jnp.where(held, seen, 0.0), axis=0, keepdims=True)

    def sums_copy(slot, other):
        return remote(sums_ref, all_sums_ref.at[slot], sums_send_sem.at[other], sums_recv_sem.at[slot], other)

    others(n, me, lambda other: sums_copy(me, other).start())
    all_sums_ref[me] = sums_ref[...]
    others(n, me, lambda other: whole(other).wait_send())
    others(n, me, lambda other: sums_copy(other, other).wait())
    mine = jnp.zeros((8, LANES), jnp.float32)
    total = jnp.zeros((8, LANES), jnp.float32)
    for row in range(n_rows):
        mine += all_sums_ref[row * tree_count + my_tree]
    for device in range(n):
        total += all_sums_ref[device]
    pooled = jnp.sum(total, axis=1, keepdims=True)
    tree_ref[...] = mine[0:1, :tree_block] / mine[1:2, :tree_block]
    forest_ref[...] = pooled[0:1] / pooled[1:2]


def forest(leaf_index, out_of_bag, labels, n_rows, tree_count):
    trees, rows = leaf_index.shape
    n = n_rows * tree_count
    tree_block = trees // tree_count
    cells = tree_block * (LEAVES // n_rows)
    vmem = pl.BlockSpec(memory_space=pltpu.VMEM)
    group_scratch = [
        pltpu.VMEM((GROUP // 2 * LEAVES * (rows // CHUNK), CHUNK), jnp.bfloat16),
        pltpu.VMEM((GROUP * (rows // LEAVES), rows), jnp.bfloat16),
        pltpu.VMEM((GROUP * 2 * LEAVES, rows), jnp.bfloat16),
    ]
    return pl.pallas_call(
        functools.partial(forest_kernel, n_rows, tree_count),
        out_shape=[
            jax.ShapeDtypeStruct((cells, pl.cdiv(CLASSES, LANES), LANES), jnp.float32),
            jax.ShapeDtypeStruct((1, tree_block), jnp.float32),
            jax.ShapeDtypeStruct((1, 1), jnp.float32),
        ],
        in_specs=[pl.BlockSpec(memory_space=pltpu.HBM)] * 3,
        out_specs=[vmem] * 3,
        scratch_shapes=[
            pltpu.VMEM((n, cells, LANES), jnp.float32),
            pltpu.VMEM((n, cells, LANES), jnp.float32),
            pltpu.VMEM((8, LANES), jnp.float32),
            pltpu.VMEM((n, 8, LANES), jnp.float32),
            pltpu.VMEM((trees, rows), jnp.float32),
            pltpu.VMEM((16, rows), jnp.bfloat16),
            pltpu.VMEM((CHUNK, CHUNK), jnp.bfloat16),
            *group_scratch,
            pltpu.VMEM((trees, rows), jnp.int32),
            pltpu.VMEM((trees, rows), jnp.bfloat16),
            pltpu.VMEM((1, rows), jnp.int32),
            pltpu.SemaphoreType.DMA((3,)),
            pltpu.SemaphoreType.DMA((n,)),
            pltpu.SemaphoreType.DMA((n,)),
            pltpu.SemaphoreType.DMA,
            pltpu.SemaphoreType.DMA((n,)),
            pltpu.SemaphoreType.DMA((n,)),
        ],
        compiler_params=pltpu.CompilerParams(
            vmem_limit_bytes=63 << 20, collective_id=0, has_side_effects=True
        ),
        name="forest",
    )(leaf_index, out_of_bag, labels.reshape(1, rows))


def per_device(leaf_index, out_of_bag, labels):
    n_rows = lax.axis_size("rows")
    tree_count = lax.axis_size("trees")
    trees = leaf_index.shape[0]
    tree_block = trees // tree_count
    leaf_block = LEAVES // n_rows
    cells = tree_block * leaf_block
    table, tree_error, pooled = forest(leaf_index, out_of_bag, labels, n_rows, tree_count)
    tallies = table.reshape(cells, -1)[:, :CLASSES].reshape(tree_block, leaf_block, CLASSES)
    return tallies, tree_error.reshape(tree_block), pooled.reshape(())


def solution(mesh):
    in_specs = (P(None, ("rows", "trees")), P(None, ("rows", "trees")), P(("rows", "trees")))
    out_specs = (P("trees", "rows", None), P("trees"), P())
    return jax.shard_map(
        per_device, mesh=mesh, in_specs=in_specs, out_specs=out_specs, check_vma=False
    )
```

```python
import functools

import jax
import jax.numpy as jnp
from jax import lax
from jax.experimental import pallas as pl
from jax.experimental.pallas import tpu as pltpu
from jax.sharding import PartitionSpec as P

CLASSES = 1000
LEAVES = 32
LANES = 128
CHUNK = 256
GROUP = 8
BATCH = 4
COUNT_STEP = 128.0


def nt_dot(a, b):
    return lax.dot_general(a, b, (((1,), (1,)), ((), ())), preferred_element_type=jnp.float32)


def rows16(row):
    return jnp.broadcast_to(row, (16, row.shape[1])).astype(jnp.bfloat16)


def ids16(first, width):
    return (lax.broadcasted_iota(jnp.int32, (16, width), 0) + first).astype(jnp.float32).astype(jnp.bfloat16)


def compact_group(group, leaf_ref, weight_ref, code_ref, tri_ref, mask_ref, hot_ref, placed_ref, first, slots):
    rows = leaf_ref.shape[1]
    chunks = rows // CHUNK
    one, zero = jnp.ones((), jnp.bfloat16), jnp.zeros((), jnp.bfloat16)
    second = jnp.full((), COUNT_STEP, jnp.bfloat16)
    leaf_ids = [ids16(q * 16, CHUNK) for q in range(LEAVES // 16)]
    slot_ids = [ids16(q * 16, CHUNK) for q in range(slots // 16)]
    leaf_ids32 = lax.broadcasted_iota(jnp.int32, (LEAVES, CHUNK), 0)
    for pair in range(group // 2):
        for c in range(chunks):
            cols = slice(c * CHUNK, (c + 1) * CHUNK)
            code = code_ref[:, cols]
            masks = []
            for j in (2 * pair, 2 * pair + 1):
                leaf = rows16(leaf_ref[pl.ds(first + j, 1), cols].astype(jnp.float32))
                weight = rows16(weight_ref[pl.ds(first + j, 1), cols])
                masks.append([leaf == ids for ids in leaf_ids])
                for q, mask in enumerate(masks[-1]):
                    at = j * 2 * LEAVES + q * 16
                    placed_ref[at:at + 16, cols] = jnp.where(mask, weight, zero)
                    placed_ref[at + LEAVES:at + LEAVES + 16, cols] = jnp.where(mask, code, zero)
            for q in range(LEAVES // 16):
                at = (pair * chunks + c) * LEAVES + q * 16
                mask_ref[at:at + 16, :] = jnp.where(masks[0][q], one, zero) + jnp.where(masks[1][q], second, zero)
    counts = jnp.dot(mask_ref[...], tri_ref[...], preferred_element_type=jnp.float32)
    for pair in range(group // 2):
        carry = jnp.zeros((LEAVES, LANES), jnp.float32)
        for c in range(chunks):
            cols = slice(c * CHUNK, (c + 1) * CHUNK)
            at = (pair * chunks + c) * LEAVES
            here = counts[at:at + LEAVES]
            running = here + jnp.concatenate([carry] * (CHUNK // LANES), axis=1)
            carry = carry + jnp.broadcast_to(here[:, CHUNK - 1:], (LEAVES, LANES))
            for side in range(2):
                j = 2 * pair + side
                mask = leaf_ref[pl.ds(first + j, 1), cols] == leaf_ids32
                both = jnp.sum(jnp.where(mask, running, 0.0), axis=0, keepdims=True)
                high = jnp.floor(both * (1.0 / COUNT_STEP))
                rank = rows16((high if side else both - high * COUNT_STEP) - 1.0)
                for q in range(slots // 16):
                    at_slot = j * slots + q * 16
                    hot_ref[at_slot:at_slot + 16, cols] = jnp.where(rank == slot_ids[q], one, zero)
    parts = []
    for base in range(0, group, BATCH):
        out = nt_dot(placed_ref[base * 2 * LEAVES:(base + BATCH) * 2 * LEAVES, :],
                     hot_ref[base * slots:(base + BATCH) * slots, :])
        for j in range(BATCH):
            mine = out[j * 2 * LEAVES:(j + 1) * 2 * LEAVES, j * slots:(j + 1) * slots]
            parts.append(jnp.concatenate([mine[:LEAVES], mine[LEAVES:]], axis=1))
    return parts


def others(n, me, body):
    lax.fori_loop(1, n, lambda k, _: body(lax.rem(me + k, n)) or 0, 0)


def greet_all(n, tree_count, me):
    barrier = pltpu.get_barrier_semaphore()

    def greet(other):
        pl.semaphore_signal(
            barrier, inc=1, device_id=(other // tree_count, lax.rem(other, tree_count)),
            device_id_type=pl.DeviceIdType.MESH,
        )

    others(n, me, greet)
    return lambda: pl.semaphore_wait(barrier, n - 1)


def add_batch(recv_ref, tally_ref, index_of, sources):
    cells = recv_ref.shape[1]
    pairs = sources // 2
    half = LANES // 2
    low_half = lax.broadcasted_iota(jnp.int32, (8, LANES), 1) < half
    lo_ids = [ids16(q * 16, LANES) for q in range(half // 16)]
    hi_ids = ids16(0, LANES)
    one, zero = jnp.ones((), jnp.bfloat16), jnp.zeros((), jnp.bfloat16)

    def step(i, _):
        at = pl.ds(pl.multiple_of(i * 8, 8), 8)
        weights, los, his = [], [], []
        for p in range(pairs):
            first, second = recv_ref[index_of(2 * p), at, :], recv_ref[index_of(2 * p + 1), at, :]
            weights.append(jnp.where(low_half, first, pltpu.roll(second, half, 1)))
            code = jnp.where(low_half, pltpu.roll(first, half, 1), second)
            power = jnp.zeros((8, LANES), jnp.int32)
            for k in range(1, -(-CLASSES // LANES)):
                power += jnp.where(code >= float(LANES << k), 1, 0)
            low = (code.astype(jnp.int32) >> power) & (LANES - 1)
            los.append((low & (half - 1)).astype(jnp.float32))
            his.append((power + (low >> 6) * 8).astype(jnp.float32))
        for j in range(8):
            a, b = [], []
            for p in range(pairs):
                low = rows16(los[p][j:j + 1])
                a.append(jnp.where(rows16(his[p][j:j + 1]) == hi_ids, rows16(weights[p][j:j + 1]), zero))
                b.append(jnp.concatenate([jnp.where(low == ids, one, zero) for ids in lo_ids], axis=0))
            table = nt_dot(jnp.concatenate(a, axis=1), jnp.concatenate(b, axis=1))
            tally_ref[i * 8 + j] += jnp.concatenate([table[:8], table[8:]], axis=1)
        return 0

    lax.fori_loop(0, cells // 8, step, 0)


def forest_kernel(n_rows, tree_count, leaf_in, bag_in, label_in, tally_ref, tree_ref, forest_ref,
                  send_ref, recv_ref, sums_ref, all_sums_ref, weight_ref, code_ref, tri_ref,
                  mask_ref, hot_ref, placed_ref, leaf_ref, bag_ref, label_ref, in_sem,
                  send_sem, recv_sem, own_sem, sums_send_sem, sums_recv_sem):
    trees, rows = leaf_ref.shape
    slots = rows // LEAVES
    leaf_block = LEAVES // n_rows
    tree_block = trees // tree_count
    cells = tree_block * leaf_block
    size = GROUP * leaf_block
    n = n_rows * tree_count
    my_row, my_tree = lax.axis_index("rows"), lax.axis_index("trees")
    me = my_row * tree_count + my_tree
    loads = [
        pltpu.make_async_copy(src, dst, in_sem.at[k])
        for k, (src, dst) in enumerate([(leaf_in, leaf_ref), (bag_in, bag_ref), (label_in, label_ref)])
    ]
    for load in loads:
        load.start()
    wait_all = greet_all(n, tree_count, me)
    tally_ref[...] = jnp.zeros_like(tally_ref)
    for load in loads:
        load.wait()

    labels = label_ref[...]
    code_ref[...] = rows16(((labels % LANES + LANES) << (labels // LANES)).astype(jnp.float32))
    r = lax.broadcasted_iota(jnp.int32, (CHUNK, CHUNK), 0)
    c = lax.broadcasted_iota(jnp.int32, (CHUNK, CHUNK), 1)
    tri_ref[...] = jnp.where(r <= c, 1.0, 0.0).astype(jnp.bfloat16)
    weight_ref[...] = bag_ref[...].astype(jnp.float32)
    wait_all()

    def remote(src, dst, sender, receiver, other):
        return pltpu.make_async_remote_copy(
            src_ref=src, dst_ref=dst, send_sem=sender, recv_sem=receiver,
            device_id=(other // tree_count, lax.rem(other, tree_count)),
            device_id_type=pl.DeviceIdType.MESH,
        )

    def piece(i, tt):
        first = tt * tree_block + i * GROUP
        parts = compact_group(GROUP, leaf_ref, weight_ref, code_ref, tri_ref,
                              mask_ref, hot_ref, placed_ref, first, slots)
        at = pl.ds(pl.multiple_of(i * size, size), size)
        for b in range(n_rows):
            tile = jnp.concatenate([p[b * leaf_block:(b + 1) * leaf_block] for p in parts], axis=0)
            send_ref[b * tree_count + tt, at, :] = tile

        def send(k, _):
            other = lax.rem(my_row + k, n_rows) * tree_count + tt

            @pl.when(other != me)
            def _():
                remote(send_ref.at[other, at], recv_ref.at[me, at], send_sem.at[other], recv_sem.at[me], other).start()

            return 0

        lax.fori_loop(0, n_rows, send, 0)

    def whole(other):
        return remote(send_ref.at[other], recv_ref.at[other], send_sem.at[other], recv_sem.at[other], other)

    own = pltpu.make_async_copy(send_ref.at[me], recv_ref.at[me], own_sem)

    def outgoing(i, _):
        tt = lax.rem(my_tree + i + 1, tree_count)
        lax.fori_loop(0, tree_block // GROUP, lambda j, _: piece(j, tt) or 0, 0)
        return 0

    lax.fori_loop(0, tree_count, outgoing, 0)
    own.start()

    def incoming(i, _):
        sender = lax.rem(my_tree + tree_count - i, tree_count)

        def arrive(row, _):
            other = row * tree_count + sender
            pl.when(other != me)(lambda: whole(other).wait_recv())
            return 0

        lax.fori_loop(0, n_rows, arrive, 0)
        pl.when(i == tree_count)(own.wait)
        add_batch(recv_ref, tally_ref, lambda row: row * tree_count + sender, n_rows)
        return 0

    lax.fori_loop(1, tree_count + 1, incoming, 0)

    table = tally_ref[...]
    seen = jnp.sum(jnp.sum(table, axis=1), axis=1, keepdims=True)
    top = jnp.max(jnp.max(table, axis=1), axis=1, keepdims=True)
    tree = lax.broadcasted_iota(jnp.int32, (cells, LANES), 0) // leaf_block
    held = tree == lax.broadcasted_iota(jnp.int32, (cells, LANES), 1)
    sums_ref[...] = jnp.zeros((8, LANES), jnp.float32)
    sums_ref[0:1] = jnp.sum(jnp.where(held, seen - top, 0.0), axis=0, keepdims=True)
    sums_ref[1:2] = jnp.sum(jnp.where(held, seen, 0.0), axis=0, keepdims=True)

    def sums_copy(slot, other):
        return remote(sums_ref, all_sums_ref.at[slot], sums_send_sem.at[other], sums_recv_sem.at[slot], other)

    others(n, me, lambda other: sums_copy(me, other).start())
    all_sums_ref[me] = sums_ref[...]
    others(n, me, lambda other: whole(other).wait_send())
    others(n, me, lambda other: sums_copy(other, other).wait())
    mine = jnp.zeros((8, LANES), jnp.float32)
    total = jnp.zeros((8, LANES), jnp.float32)
    for row in range(n_rows):
        mine += all_sums_ref[row * tree_count + my_tree]
    for device in range(n):
        total += all_sums_ref[device]
    pooled = jnp.sum(total, axis=1, keepdims=True)
    tree_ref[...] = mine[0:1, :tree_block] / mine[1:2, :tree_block]
    forest_ref[...] = pooled[0:1] / pooled[1:2]


def forest(leaf_index, out_of_bag, labels, n_rows, tree_count):
    trees, rows = leaf_index.shape
    n = n_rows * tree_count
    tree_block = trees // tree_count
    cells = tree_block * (LEAVES // n_rows)
    vmem = pl.BlockSpec(memory_space=pltpu.VMEM)
    group_scratch = [
        pltpu.VMEM((GROUP // 2 * LEAVES * (rows // CHUNK), CHUNK), jnp.bfloat16),
        pltpu.VMEM((GROUP * (rows // LEAVES), rows), jnp.bfloat16),
        pltpu.VMEM((GROUP * 2 * LEAVES, rows), jnp.bfloat16),
    ]
    return pl.pallas_call(
        functools.partial(forest_kernel, n_rows, tree_count),
        out_shape=[
            jax.ShapeDtypeStruct((cells, pl.cdiv(CLASSES, LANES), LANES), jnp.float32),
            jax.ShapeDtypeStruct((1, tree_block), jnp.float32),
            jax.ShapeDtypeStruct((1, 1), jnp.float32),
        ],
        in_specs=[pl.BlockSpec(memory_space=pltpu.HBM)] * 3,
        out_specs=[vmem] * 3,
        scratch_shapes=[
            pltpu.VMEM((n, cells, LANES), jnp.float32),
            pltpu.VMEM((n, cells, LANES), jnp.float32),
            pltpu.VMEM((8, LANES), jnp.float32),
            pltpu.VMEM((n, 8, LANES), jnp.float32),
            pltpu.VMEM((trees, rows), jnp.float32),
            pltpu.VMEM((16, rows), jnp.bfloat16),
            pltpu.VMEM((CHUNK, CHUNK), jnp.bfloat16),
            *group_scratch,
            pltpu.VMEM((trees, rows), jnp.int32),
            pltpu.VMEM((trees, rows), jnp.bfloat16),
            pltpu.VMEM((1, rows), jnp.int32),
            pltpu.SemaphoreType.DMA((3,)),
            pltpu.SemaphoreType.DMA((n,)),
            pltpu.SemaphoreType.DMA((n,)),
            pltpu.SemaphoreType.DMA,
            pltpu.SemaphoreType.DMA((n,)),
            pltpu.SemaphoreType.DMA((n,)),
        ],
        compiler_params=pltpu.CompilerParams(
            vmem_limit_bytes=63 << 20, collective_id=0, has_side_effects=True
        ),
        name="forest",
    )(leaf_index, out_of_bag, labels.reshape(1, rows))


def per_device(leaf_index, out_of_bag, labels):
    n_rows = lax.axis_size("rows")
    tree_count = lax.axis_size("trees")
    trees = leaf_index.shape[0]
    tree_block = trees // tree_count
    leaf_block = LEAVES // n_rows
    cells = tree_block * leaf_block
    table, tree_error, pooled = forest(leaf_index, out_of_bag, labels, n_rows, tree_count)
    tallies = table.reshape(cells, -1)[:, :CLASSES].reshape(tree_block, leaf_block, CLASSES)
    return tallies, tree_error.reshape(tree_block), pooled.reshape(())


def solution(mesh):
    in_specs = (P(None, ("rows", "trees")), P(None, ("rows", "trees")), P(("rows", "trees")))
    out_specs = (P("trees", "rows", None), P("trees"), P())
    return jax.shard_map(
        per_device, mesh=mesh, in_specs=in_specs, out_specs=out_specs, check_vma=False
    )
```

```python
import functools

import jax
import jax.numpy as jnp
from jax import lax
from jax.experimental import pallas as pl
from jax.experimental.pallas import tpu as pltpu
from jax.sharding import PartitionSpec as P

CLASSES = 1000
LEAVES = 32
LANES = 128
CHUNK = 256
GROUP = 8
BATCH = 4
COUNT_STEP = 128.0


def nt_dot(a, b):
    return lax.dot_general(a, b, (((1,), (1,)), ((), ())), preferred_element_type=jnp.float32)


def rows16(row):
    return jnp.broadcast_to(row, (16, row.shape[1])).astype(jnp.bfloat16)


def ids16(first, width):
    return (lax.broadcasted_iota(jnp.int32, (16, width), 0) + first).astype(jnp.float32).astype(jnp.bfloat16)


def compact_group(group, leaf_ref, weight_ref, code_ref, tri_ref, mask_ref, hot_ref, placed_ref, first, slots):
    rows = leaf_ref.shape[1]
    chunks = rows // CHUNK
    one, zero = jnp.ones((), jnp.bfloat16), jnp.zeros((), jnp.bfloat16)
    second = jnp.full((), COUNT_STEP, jnp.bfloat16)
    leaf_ids = [ids16(q * 16, CHUNK) for q in range(LEAVES // 16)]
    slot_ids = [ids16(q * 16, CHUNK) for q in range(slots // 16)]
    leaf_ids32 = lax.broadcasted_iota(jnp.int32, (LEAVES, CHUNK), 0)
    for pair in range(group // 2):
        for c in range(chunks):
            cols = slice(c * CHUNK, (c + 1) * CHUNK)
            code = code_ref[:, cols]
            masks = []
            for j in (2 * pair, 2 * pair + 1):
                leaf = rows16(leaf_ref[pl.ds(first + j, 1), cols].astype(jnp.float32))
                weight = rows16(weight_ref[pl.ds(first + j, 1), cols])
                masks.append([leaf == ids for ids in leaf_ids])
                for q, mask in enumerate(masks[-1]):
                    at = j * 2 * LEAVES + q * 16
                    placed_ref[at:at + 16, cols] = jnp.where(mask, weight, zero)
                    placed_ref[at + LEAVES:at + LEAVES + 16, cols] = jnp.where(mask, code, zero)
            for q in range(LEAVES // 16):
                at = (pair * chunks + c) * LEAVES + q * 16
                mask_ref[at:at + 16, :] = jnp.where(masks[0][q], one, zero) + jnp.where(masks[1][q], second, zero)
    counts = jnp.dot(mask_ref[...], tri_ref[...], preferred_element_type=jnp.float32)
    for pair in range(group // 2):
        carry = jnp.zeros((LEAVES, LANES), jnp.float32)
        for c in range(chunks):
            cols = slice(c * CHUNK, (c + 1) * CHUNK)
            at = (pair * chunks + c) * LEAVES
            here = counts[at:at + LEAVES]
            running = here + jnp.concatenate([carry] * (CHUNK // LANES), axis=1)
            carry = carry + jnp.broadcast_to(here[:, CHUNK - 1:], (LEAVES, LANES))
            for side in range(2):
                j = 2 * pair + side
                mask = leaf_ref[pl.ds(first + j, 1), cols] == leaf_ids32
                both = jnp.sum(jnp.where(mask, running, 0.0), axis=0, keepdims=True)
                high = jnp.floor(both * (1.0 / COUNT_STEP))
                rank = rows16((high if side else both - high * COUNT_STEP) - 1.0)
                for q in range(slots // 16):
                    at_slot = j * slots + q * 16
                    hot_ref[at_slot:at_slot + 16, cols] = jnp.where(rank == slot_ids[q], one, zero)
    parts = []
    for base in range(0, group, BATCH):
        out = nt_dot(placed_ref[base * 2 * LEAVES:(base + BATCH) * 2 * LEAVES, :],
                     hot_ref[base * slots:(base + BATCH) * slots, :])
        for j in range(BATCH):
            mine = out[j * 2 * LEAVES:(j + 1) * 2 * LEAVES, j * slots:(j + 1) * slots]
            parts.append(jnp.concatenate([mine[:LEAVES], mine[LEAVES:]], axis=1))
    return parts


def others(n, me, body):
    lax.fori_loop(1, n, lambda k, _: body(lax.rem(me + k, n)) or 0, 0)


def greet_all(n, tree_count, me):
    barrier = pltpu.get_barrier_semaphore()

    def greet(other):
        pl.semaphore_signal(
            barrier, inc=1, device_id=(other // tree_count, lax.rem(other, tree_count)),
            device_id_type=pl.DeviceIdType.MESH,
        )

    others(n, me, greet)
    return lambda: pl.semaphore_wait(barrier, n - 1)


def add_batch(recv_ref, tally_ref, index_of, sources):
    cells = recv_ref.shape[1]
    pairs = sources // 2
    half = LANES // 2
    low_half = lax.broadcasted_iota(jnp.int32, (8, LANES), 1) < half
    lo_ids = [ids16(q * 16, LANES) for q in range(half // 16)]
    hi_ids = ids16(0, LANES)
    one, zero = jnp.ones((), jnp.bfloat16), jnp.zeros((), jnp.bfloat16)

    def step(i, _):
        at = pl.ds(pl.multiple_of(i * 8, 8), 8)
        weights, los, his = [], [], []
        for p in range(pairs):
            first, second = recv_ref[index_of(2 * p), at, :], recv_ref[index_of(2 * p + 1), at, :]
            weights.append(jnp.where(low_half, first, pltpu.roll(second, half, 1)))
            code = jnp.where(low_half, pltpu.roll(first, half, 1), second)
            power = jnp.zeros((8, LANES), jnp.int32)
            for k in range(1, -(-CLASSES // LANES)):
                power += jnp.where(code >= float(LANES << k), 1, 0)
            low = (code.astype(jnp.int32) >> power) & (LANES - 1)
            los.append((low & (half - 1)).astype(jnp.float32))
            his.append((power + (low >> 6) * 8).astype(jnp.float32))
        for j in range(8):
            a, b = [], []
            for p in range(pairs):
                low = rows16(los[p][j:j + 1])
                a.append(jnp.where(rows16(his[p][j:j + 1]) == hi_ids, rows16(weights[p][j:j + 1]), zero))
                b.append(jnp.concatenate([jnp.where(low == ids, one, zero) for ids in lo_ids], axis=0))
            table = nt_dot(jnp.concatenate(a, axis=1), jnp.concatenate(b, axis=1))
            tally_ref[i * 8 + j] += jnp.concatenate([table[:8], table[8:]], axis=1)
        return 0

    lax.fori_loop(0, cells // 8, step, 0)


def forest_kernel(n_rows, tree_count, leaf_in, bag_in, label_in, tally_ref, tree_ref, forest_ref,
                  send_ref, recv_ref, sums_ref, all_sums_ref, weight_ref, code_ref, tri_ref,
                  mask_ref, hot_ref, placed_ref, leaf_ref, bag_ref, label_ref, in_sem,
                  send_sem, recv_sem, own_sem, sums_send_sem, sums_recv_sem):
    trees, rows = leaf_ref.shape
    slots = rows // LEAVES
    leaf_block = LEAVES // n_rows
    tree_block = trees // tree_count
    cells = tree_block * leaf_block
    size = GROUP * leaf_block
    n = n_rows * tree_count
    my_row, my_tree = lax.axis_index("rows"), lax.axis_index("trees")
    me = my_row * tree_count + my_tree
    loads = [
        pltpu.make_async_copy(src, dst, in_sem.at[k])
        for k, (src, dst) in enumerate([(leaf_in, leaf_ref), (bag_in, bag_ref), (label_in, label_ref)])
    ]
    for load in loads:
        load.start()
    wait_all = greet_all(n, tree_count, me)
    tally_ref[...] = jnp.zeros_like(tally_ref)
    for load in loads:
        load.wait()

    labels = label_ref[...]
    code_ref[...] = rows16(((labels % LANES + LANES) << (labels // LANES)).astype(jnp.float32))
    r = lax.broadcasted_iota(jnp.int32, (CHUNK, CHUNK), 0)
    c = lax.broadcasted_iota(jnp.int32, (CHUNK, CHUNK), 1)
    tri_ref[...] = jnp.where(r <= c, 1.0, 0.0).astype(jnp.bfloat16)
    weight_ref[...] = bag_ref[...].astype(jnp.float32)
    wait_all()

    def remote(src, dst, sender, receiver, other):
        return pltpu.make_async_remote_copy(
            src_ref=src, dst_ref=dst, send_sem=sender, recv_sem=receiver,
            device_id=(other // tree_count, lax.rem(other, tree_count)),
            device_id_type=pl.DeviceIdType.MESH,
        )

    def piece(i, tt):
        first = tt * tree_block + i * GROUP
        parts = compact_group(GROUP, leaf_ref, weight_ref, code_ref, tri_ref,
                              mask_ref, hot_ref, placed_ref, first, slots)
        at = pl.ds(pl.multiple_of(i * size, size), size)
        for b in range(n_rows):
            tile = jnp.concatenate([p[b * leaf_block:(b + 1) * leaf_block] for p in parts], axis=0)
            send_ref[b * tree_count + tt, at, :] = tile

        def send(k, _):
            other = lax.rem(my_row + n_rows // 2 + k, n_rows) * tree_count + tt

            @pl.when(other != me)
            def _():
                remote(send_ref.at[other, at], recv_ref.at[me, at], send_sem.at[other], recv_sem.at[me], other).start()

            return 0

        lax.fori_loop(0, n_rows, send, 0)

    def whole(other):
        return remote(send_ref.at[other], recv_ref.at[other], send_sem.at[other], recv_sem.at[other], other)

    own = pltpu.make_async_copy(send_ref.at[me], recv_ref.at[me], own_sem)

    def outgoing(i, _):
        tt = lax.rem(my_tree + i + 1, tree_count)
        lax.fori_loop(0, tree_block // GROUP, lambda j, _: piece(j, tt) or 0, 0)
        return 0

    lax.fori_loop(0, tree_count, outgoing, 0)
    own.start()

    def incoming(i, _):
        sender = lax.rem(my_tree + tree_count - i, tree_count)

        def arrive(row, _):
            other = row * tree_count + sender
            pl.when(other != me)(lambda: whole(other).wait_recv())
            return 0

        lax.fori_loop(0, n_rows, arrive, 0)
        pl.when(i == tree_count)(own.wait)
        add_batch(recv_ref, tally_ref, lambda row: row * tree_count + sender, n_rows)
        return 0

    lax.fori_loop(1, tree_count + 1, incoming, 0)

    table = tally_ref[...]
    seen = jnp.sum(jnp.sum(table, axis=1), axis=1, keepdims=True)
    top = jnp.max(jnp.max(table, axis=1), axis=1, keepdims=True)
    tree = lax.broadcasted_iota(jnp.int32, (cells, LANES), 0) // leaf_block
    held = tree == lax.broadcasted_iota(jnp.int32, (cells, LANES), 1)
    sums_ref[...] = jnp.zeros((8, LANES), jnp.float32)
    sums_ref[0:1] = jnp.sum(jnp.where(held, seen - top, 0.0), axis=0, keepdims=True)
    sums_ref[1:2] = jnp.sum(jnp.where(held, seen, 0.0), axis=0, keepdims=True)

    def sums_copy(slot, other):
        return remote(sums_ref, all_sums_ref.at[slot], sums_send_sem.at[other], sums_recv_sem.at[slot], other)

    others(n, me, lambda other: sums_copy(me, other).start())
    all_sums_ref[me] = sums_ref[...]
    others(n, me, lambda other: whole(other).wait_send())
    others(n, me, lambda other: sums_copy(other, other).wait())
    mine = jnp.zeros((8, LANES), jnp.float32)
    total = jnp.zeros((8, LANES), jnp.float32)
    for row in range(n_rows):
        mine += all_sums_ref[row * tree_count + my_tree]
    for device in range(n):
        total += all_sums_ref[device]
    pooled = jnp.sum(total, axis=1, keepdims=True)
    tree_ref[...] = mine[0:1, :tree_block] / mine[1:2, :tree_block]
    forest_ref[...] = pooled[0:1] / pooled[1:2]


def forest(leaf_index, out_of_bag, labels, n_rows, tree_count):
    trees, rows = leaf_index.shape
    n = n_rows * tree_count
    tree_block = trees // tree_count
    cells = tree_block * (LEAVES // n_rows)
    vmem = pl.BlockSpec(memory_space=pltpu.VMEM)
    group_scratch = [
        pltpu.VMEM((GROUP // 2 * LEAVES * (rows // CHUNK), CHUNK), jnp.bfloat16),
        pltpu.VMEM((GROUP * (rows // LEAVES), rows), jnp.bfloat16),
        pltpu.VMEM((GROUP * 2 * LEAVES, rows), jnp.bfloat16),
    ]
    return pl.pallas_call(
        functools.partial(forest_kernel, n_rows, tree_count),
        out_shape=[
            jax.ShapeDtypeStruct((cells, pl.cdiv(CLASSES, LANES), LANES), jnp.float32),
            jax.ShapeDtypeStruct((1, tree_block), jnp.float32),
            jax.ShapeDtypeStruct((1, 1), jnp.float32),
        ],
        in_specs=[pl.BlockSpec(memory_space=pltpu.HBM)] * 3,
        out_specs=[vmem] * 3,
        scratch_shapes=[
            pltpu.VMEM((n, cells, LANES), jnp.float32),
            pltpu.VMEM((n, cells, LANES), jnp.float32),
            pltpu.VMEM((8, LANES), jnp.float32),
            pltpu.VMEM((n, 8, LANES), jnp.float32),
            pltpu.VMEM((trees, rows), jnp.float32),
            pltpu.VMEM((16, rows), jnp.bfloat16),
            pltpu.VMEM((CHUNK, CHUNK), jnp.bfloat16),
            *group_scratch,
            pltpu.VMEM((trees, rows), jnp.int32),
            pltpu.VMEM((trees, rows), jnp.bfloat16),
            pltpu.VMEM((1, rows), jnp.int32),
            pltpu.SemaphoreType.DMA((3,)),
            pltpu.SemaphoreType.DMA((n,)),
            pltpu.SemaphoreType.DMA((n,)),
            pltpu.SemaphoreType.DMA,
            pltpu.SemaphoreType.DMA((n,)),
            pltpu.SemaphoreType.DMA((n,)),
        ],
        compiler_params=pltpu.CompilerParams(
            vmem_limit_bytes=63 << 20, collective_id=0, has_side_effects=True
        ),
        name="forest",
    )(leaf_index, out_of_bag, labels.reshape(1, rows))


def per_device(leaf_index, out_of_bag, labels):
    n_rows = lax.axis_size("rows")
    tree_count = lax.axis_size("trees")
    trees = leaf_index.shape[0]
    tree_block = trees // tree_count
    leaf_block = LEAVES // n_rows
    cells = tree_block * leaf_block
    table, tree_error, pooled = forest(leaf_index, out_of_bag, labels, n_rows, tree_count)
    tallies = table.reshape(cells, -1)[:, :CLASSES].reshape(tree_block, leaf_block, CLASSES)
    return tallies, tree_error.reshape(tree_block), pooled.reshape(())


def solution(mesh):
    in_specs = (P(None, ("rows", "trees")), P(None, ("rows", "trees")), P(("rows", "trees")))
    out_specs = (P("trees", "rows", None), P("trees"), P())
    return jax.shard_map(
        per_device, mesh=mesh, in_specs=in_specs, out_specs=out_specs, check_vma=False
    )
```
